256 devices in a mesh: section: 2 (over z_lo), dp: 128 (over x, y, z_hi, core).
Axes of the slice: x: 4, y: 4, z: 8 (z_hi: 4, z_lo: 2; z = z_hi * 2 + z_lo), core: 2. Of those that a mesh axis runs over, the one named last changes fastest.
Arguments:
- tokens: bfloat16 [98304, 832], P('dp'), may hold values from -6 to 6
- out_grad: bfloat16 [98304, 832], P('dp'), may hold values from -0.059814453 to 0.059814453
- boundary: int32 [1], replicated, may hold values from 0 to 11
- up_old: float32 [12, 2, 832, 2048], P('section', None, None, 'dp'), may hold values from -0.21875 to 0.21875
- down_old: float32 [12, 2, 2048, 832], P('section', None, 'dp'), may hold values from -0.09375 to 0.09375
- up_mom: float32 [12, 2, 832, 2048], P('section', None, None, 'dp'), may hold values from -2 to 2
- up_var: float32 [12, 2, 832, 2048], P('section', None, None, 'dp'), may hold values from 0.01 to 1
- down_mom: float32 [12, 2, 2048, 832], P('section', None, 'dp'), may hold values from -2 to 2
- down_var: float32 [12, 2, 2048, 832], P('section', None, 'dp'), may hold values from 0.01 to 1
Outputs:
- mixed: bfloat16 [98304, 832], P('dp')
- up_new: float32 [2, 832, 2048], P('section', None, 'dp')
- up_mom_new: float32 [2, 832, 2048], P('section', None, 'dp')
- up_var_new: float32 [2, 832, 2048], P('section', None, 'dp')
- down_new: float32 [2, 2048, 832], P('section', 'dp')
- down_mom_new: float32 [2, 2048, 832], P('section', 'dp')
- down_var_new: float32 [2, 2048, 832], P('section', 'dp')
The draws below stay inside these ranges and needn't reach their ends.
All inputs are finite; a program needn't handle non-finite values.
Results may differ from the reference program's by a relative error of at most 0.00115.
The reference program's roundings to bfloat16 on the way (of `normed`, `act` and `slope`) count: a program that leaves them out, or rounds other values in their place, can miss the bound.
Values may be sent and summed in bfloat16 or wider, within the bound.
A program may use at most 128 MiB of HBM per device.

```python
import math
import jax
import jax.numpy as jnp
from jax import lax

D = 832
FF = 4096
TOK_DEV = 768
HALF = 2048
LAYERS = 12
TOKENS = 98304


def levels(rng, extent, pieces, smallest, top_value):
    def one(axis_at, shards_of):
        heights = jax.random.uniform(jax.random.fold_in(jax.random.fold_in(rng, 6), axis_at), (shards_of,), jnp.float32, smallest / len(pieces), top_value / len(pieces))
        return jnp.repeat(jnp.exp(heights), extent[axis_at] // shards_of).reshape((-1,) + (1,) * (len(extent) - axis_at - 1))

    level = one(*pieces[0])
    for cut in pieces[1:]:
        level = level * one(*cut)
    return level


def noise(rng, dims, scale, limit, split=(), kind=jnp.bfloat16):
    values = scale * jax.random.normal(rng, dims, jnp.float32)
    if split:
        values = values * levels(rng, dims, split, -0.22, 0.18)
    return jnp.clip(values, -limit, limit).astype(kind)


def setup_inputs(seed: int = 0) -> dict:
    key_of = jax.random.split(jax.random.key(seed), 10)
    tokens = noise(key_of[0], (TOKENS, D), 1.0, 6.0, ((0, 128),))
    out_grad = noise(key_of[1], (TOKENS, D), 0.01, 0.059814453, ((0, 128),))
    boundary = jax.random.randint(key_of[2], (1,), 0, LAYERS).astype(jnp.int32)
    up_old = noise(key_of[3], (LAYERS, 2, D, HALF), D ** -0.5, 0.21875, ((0, 2), (3, 128)), jnp.float32)
    down_old = noise(key_of[4], (LAYERS, 2, HALF, D), FF ** -0.5, 0.09375, ((0, 2), (2, 128)), jnp.float32)
    up_mom = noise(key_of[5], (LAYERS, 2, D, HALF), 0.3, 2.0, ((0, 2), (3, 128)), jnp.float32)
    up_var = jnp.clip(jnp.exp(math.log(1.0) - 4.6051702 * jax.random.uniform(key_of[6], (LAYERS, 2, D, HALF), jnp.float32) ** levels(key_of[6], (LAYERS, 2, D, HALF), ((0, 2), (3, 128)), -0.2, 0.2)), 0.01, 1.0)
    down_mom = noise(key_of[7], (LAYERS, 2, HALF, D), 0.3, 2.0, ((0, 2), (2, 128)), jnp.float32)
    down_var = jnp.clip(jnp.exp(math.log(1.0) - 4.6051702 * jax.random.uniform(key_of[8], (LAYERS, 2, HALF, D), jnp.float32) ** levels(key_of[8], (LAYERS, 2, HALF, D), ((0, 2), (2, 128)), -0.2, 0.2)), 0.01, 1.0)
    return dict(tokens=tokens, out_grad=out_grad, boundary=boundary, up_old=up_old, down_old=down_old, up_mom=up_mom, up_var=up_var, down_mom=down_mom, down_var=down_var)


root_half = 1.0 / math.sqrt(2.0)
root_circle = 1.0 / math.sqrt(2.0 * math.pi)
first_fix = 1.0 - 0.9 ** 10
second_fix = 1.0 - 0.999 ** 10

def gelu_value(value):
    return 0.5 * value * (1.0 + lax.erf(value * root_half))

def gelu_slope(value):
    return 0.5 * (1.0 + lax.erf(value * root_half)) + value * jnp.exp(-0.5 * value * value) * root_circle

def layer_norm(tokens):
    wide = tokens.astype(jnp.float32)
    center = wide - lax.optimization_barrier(jnp.mean(wide, axis=1, keepdims=True))
    spread = lax.optimization_barrier(jnp.mean(center * center, axis=1, keepdims=True))
    return (center * lax.rsqrt(spread + 1e-06)).astype(jnp.bfloat16)

def adam_update(weight, moment, second, grad):
    moment_new = 0.9 * moment + 0.1 * grad
    second_new = 0.999 * second + 0.001 * grad * grad
    stride = moment_new / first_fix / (jnp.sqrt(second_new / second_fix) + 1e-08)
    return (weight - 0.001 * stride, moment_new, second_new)

def reference(tokens, out_grad, boundary, up_old, down_old, up_mom, up_var, down_mom, down_var):
    active = boundary[0].astype(jnp.int32)

    def pick(array):
        return lax.dynamic_index_in_dim(array, active, 0, keepdims=False)
    up_w, up_m, up_v = (pick(up_old), pick(up_mom), pick(up_var))
    down_w, down_m, down_v = (pick(down_old), pick(down_mom), pick(down_var))
    up_full = jnp.concatenate([up_w[0], up_w[1]], axis=1).astype(jnp.bfloat16)
    down_full = down_w.reshape(FF, D).astype(jnp.bfloat16)
    blocks = TOKENS // TOK_DEV
    token_blocks = tokens.reshape(blocks, TOK_DEV, D)
    grad_blocks = out_grad.reshape(blocks, TOK_DEV, D)

    def stepper(carry, inputs):
        sum_up, sum_down = carry
        block_tokens, block_grad = inputs
        normed = layer_norm(block_tokens)
        pre = jnp.dot(normed, up_full, preferred_element_type=jnp.float32)
        act = gelu_value(pre).astype(jnp.bfloat16)
        branch = jnp.dot(act, down_full, preferred_element_type=jnp.float32)
        mixed = (block_tokens.astype(jnp.float32) + branch).astype(jnp.bfloat16)
        back = lax.dot_general(block_grad, down_full, (((1,), (1,)), ((), ())), preferred_element_type=jnp.float32)
        slope = (back * gelu_slope(pre)).astype(jnp.bfloat16)
        sum_up = sum_up + lax.dot_general(normed, slope, (((0,), (0,)), ((), ())), preferred_element_type=jnp.float32)
        sum_down = sum_down + lax.dot_general(act, block_grad, (((0,), (0,)), ((), ())), preferred_element_type=jnp.float32)
        return ((sum_up, sum_down), mixed)
    start = (jnp.zeros((D, FF), jnp.float32), jnp.zeros((FF, D), jnp.float32))
    (sum_up, sum_down), mixed = lax.scan(stepper, start, (token_blocks, grad_blocks))
    mixed = mixed.reshape(TOKENS, D)
    grad_up = jnp.stack([sum_up[:, :HALF], sum_up[:, HALF:]], axis=0)
    grad_down = sum_down.reshape(2, HALF, D)
    up_new, up_mom_new, up_var_new = adam_update(up_w, up_m, up_v, grad_up)
    down_new, down_mom_new, down_var_new = adam_update(down_w, down_m, down_v, grad_down)
    return (mixed, up_new, up_mom_new, up_var_new, down_new, down_mom_new, down_var_new)
```

```python
import functools
import math

import jax
import jax.numpy as jnp
from jax import lax
from jax.experimental import pallas as pl
from jax.experimental.pallas import tpu as pltpu
from jax.sharding import PartitionSpec as P

root_half = 1.0 / math.sqrt(2.0)
root_circle = 1.0 / math.sqrt(2.0 * math.pi)
first_fix = 1.0 - 0.9**10
second_fix = 1.0 - 0.999**10

D = 832
ROWS = 16
TOK = 768
HALF_TOK = TOK // 2
UNITS = 64 * ROWS
CLASS = 16 * ROWS
F32 = jnp.float32
BF16 = jnp.bfloat16


def dot(a, b, ca, cb):
    return lax.dot_general(a, b, (((ca,), (cb,)), ((), ())), preferred_element_type=F32)


def gelu_both(value):
    both = 1.0 + lax.erf(value * root_half)
    return 0.5 * value * both, 0.5 * both + value * jnp.exp(-0.5 * value * value) * root_circle


def layer_norm(tokens):
    wide = tokens.astype(F32)
    center = wide - jnp.mean(wide, axis=0, keepdims=True)
    spread = jnp.mean(center * center, axis=0, keepdims=True)
    return (center * lax.rsqrt(spread + 1e-06)).astype(BF16)


def adam_update(weight, moment, second, grad):
    moment_new = 0.9 * moment + 0.1 * grad
    second_new = 0.999 * second + 0.001 * grad * grad
    stride = moment_new / first_fix / (jnp.sqrt(second_new / second_fix) + 1e-08)
    return (weight - 0.001 * stride, moment_new, second_new)


def flip1(v):
    return v + 1 - 2 * lax.rem(v, 2)


def flip2(v):
    return lax.rem(v + 2, 4)


def flip3(v):
    return 3 - v


def kernel(
    boundary,
    tok_in,
    og_in,
    up_w_in,
    down_w_in,
    up_m_in,
    up_v_in,
    down_m_in,
    down_v_in,
    mixed_out,
    up_w_out,
    up_m_out,
    up_v_out,
    down_w_out,
    down_m_out,
    down_v_out,
    up_w,
    down_w,
    up_m,
    down_m,
    up_v,
    down_v,
    pick_send,
    pick_recv,
    picked,
    tok,
    nrm,
    og,
    w1,
    w2,
    act,
    gate,
    slope,
    psend,
    pown,
    precv,
    zrecv,
    mix,
    gd,
    gu,
    rd,
    ru,
    zd,
    zu,
    local_sem,
    send_sem,
    recv_sem,
):
    s = lax.axis_index("section")
    d = lax.axis_index("dp")
    x, y, z, c = lax.div(d, 32), lax.rem(lax.div(d, 8), 4), lax.rem(lax.div(d, 2), 4), lax.rem(d, 2)
    core = {"dp": d + 1 - 2 * c}
    pair = {"section": 1 - s}
    xy = (
        {"dp": d + (flip1(x) - x) * 32},
        {"dp": d + (flip3(x) - x) * 32},
        {"dp": d + (flip1(y) - y) * 8},
        {"dp": d + (flip3(y) - y) * 8},
    )
    zs = (
        {"dp": d + (flip1(z) - z) * 2},
        {"dp": d + (flip3(z) - z) * 2},
        {"dp": d + (flip2(z) - z) * 2},
    )
    state = (up_w, down_w, up_m, down_m, up_v, down_v)
    active = boundary[0]
    slot = lax.rem(active, 6)
    owner = lax.div(active, 6)

    count = [0]
    started = []

    def send(src, dst, dev):
        i = count[0]
        count[0] += 1
        copy = pltpu.make_async_remote_copy(
            src_ref=src,
            dst_ref=dst,
            send_sem=send_sem.at[i],
            recv_sem=recv_sem.at[i],
            device_id=dev,
            device_id_type=pl.DeviceIdType.MESH,
        )
        copy.start()
        started.append(copy)
        return copy

    mine = pl.ds(pl.multiple_of(s * HALF_TOK, 128), HALF_TOK)
    other = pl.ds(pl.multiple_of((1 - s) * HALF_TOK, 128), HALF_TOK)
    first, second = pl.ds(0, HALF_TOK), pl.ds(HALF_TOK, HALF_TOK)

    def fetch(i, src, dst):
        copy = pltpu.make_async_copy(src, dst, local_sem.at[i])
        copy.start()
        return copy

    get_w = [fetch(0, up_w_in, up_w), fetch(1, down_w_in, down_w)]
    get_tok = [
        fetch(2, tok_in.at[:, mine], tok.at[:, first]),
        fetch(3, tok_in.at[:, other], tok.at[:, second]),
    ]
    get_og = [
        fetch(4, og_in.at[:, mine], og.at[:, pl.ds(0, HALF_TOK)]),
        fetch(5, og_in.at[:, other], og.at[:, pl.ds(HALF_TOK, HALF_TOK)]),
    ]
    get_mv = [
        fetch(6, up_m_in, up_m),
        fetch(7, down_m_in, down_m),
        fetch(8, up_v_in, up_v),
        fetch(9, down_v_in, down_v),
    ]

    barrier = pltpu.get_barrier_semaphore()
    peers = (core, pair) + xy + zs
    for peer in peers:
        pl.semaphore_signal(barrier, inc=1, device_id=peer, device_id_type=pl.DeviceIdType.MESH)
    pl.semaphore_wait(barrier, len(peers))

    def swap(i):
        pick_send[i] = state[i][slot, 1 - s]
        return send(pick_send.at[i], pick_recv.at[i], pair)

    def settle(i, copy):
        copy.wait_recv()
        picked[i] = jnp.where(owner == s, state[i][slot, s], pick_recv[i])

    for copy in get_w:
        copy.wait()
    moved = [swap(0), swap(1)]
    for copy in get_og:
        copy.wait()
    og_swap = send(og.at[:, pl.ds(0, TOK)], og.at[:, pl.ds(TOK, TOK)], core)
    for copy in get_tok:
        copy.wait()

    def norm_half(h):
        @pl.loop(0, HALF_TOK // 128)
        def _(i):
            at = pl.ds(pl.multiple_of(h * HALF_TOK + i * 128, 128), 128)
            nrm[:, at] = layer_norm(tok[:, at])

    norm_half(0)
    weights = (w1, w2)
    gathered = {}
    for m in (0, 1):
        settle(m, moved[m])
        weights[m][pl.ds(0, ROWS), :] = picked[m].astype(BF16)
        for q in (1, 2, 3):
            gathered[m, q, -1] = send(
                weights[m].at[pl.ds(0, ROWS), :], weights[m].at[pl.ds(q * CLASS, ROWS), :], zs[q - 1]
            )
    norm_half(1)
    nrm_swap = send(nrm.at[:, pl.ds(0, TOK)], nrm.at[:, pl.ds(TOK, TOK)], core)

    for j in range(4):
        n = ROWS << j
        for m in (0, 1):
            for q in range(4):
                if j > 0 or q > 0:
                    gathered[m, q, j - 1].wait_recv()
                gathered[m, q, j] = send(
                    weights[m].at[pl.ds(q * CLASS, n), :],
                    weights[m].at[pl.ds(q * CLASS + n, n), :],
                    xy[(q + j) % 4],
                )
        if j == 0:
            for copy in get_mv:
                copy.wait()
            moved += [swap(i) for i in (2, 3, 4, 5)]

    og_swap.wait_recv()
    nrm_swap.wait_recv()
    for q in range(4):
        gathered[0, q, 3].wait_recv()

    def forward(t):
        cols = pl.ds(t * TOK, TOK)

        @pl.loop(0, 2)
        def _(i):
            rows = pl.ds(pl.multiple_of(i * 512, 512), 512)
            value, rate = gelu_both(dot(w1[rows, :], nrm[:, cols], 1, 0))
            act[rows, cols] = value.astype(BF16)
            gate[rows, cols] = rate

    forward(1)
    for q in range(4):
        gathered[1, q, 3].wait_recv()

    def branch(block):
        return dot(w2[...], act[:, pl.ds(block * HALF_TOK, HALF_TOK)], 0, 0)

    psend[1] = branch(3)
    core_swap1 = send(psend.at[1], precv.at[1], core)
    psend[0] = branch(2)
    core_swap0 = send(psend.at[0], precv.at[0], core)
    forward(0)
    pown[1] = branch(1)
    core_swap1.wait_recv()
    pown[1] += precv[1]
    pair_swap = send(pown.at[1], zrecv, pair)

    sums = {}

    def begin(name, grad, recv, q):
        top = CLASS // 2
        sums[name, q, 3] = send(
            grad.at[pl.ds(q * CLASS + top, top), :], recv.at[pl.ds(q * 240, top), :], xy[(q + 3) % 4]
        )

    def advance(name, grad, recv, zrecv_, j):
        n = ROWS << j
        at = (16 - (2 << j)) * ROWS
        for q in range(4):
            base, low = q * CLASS, q * 240 + at
            sums[name, q, j].wait_recv()
            if j > 0:
                h = n // 2
                grad[pl.ds(base + h, h), :] += recv[pl.ds(low + h, h), :]
                sums[name, q, j - 1] = send(
                    grad.at[pl.ds(base + h, h), :],
                    recv.at[pl.ds(low + n, h), :],
                    xy[(q + j - 1) % 4],
                )
                grad[pl.ds(base, h), :] += recv[pl.ds(low, h), :]
            else:
                grad[pl.ds(base, n), :] += recv[pl.ds(low, n), :]
                if q > 0:
                    sums[name, q, -1] = send(grad.at[pl.ds(base, n), :], zrecv_.at[q - 1], zs[q - 1])

    def finish(name, grad, zrecv_):
        total = grad[pl.ds(0, ROWS), :]
        for q in (1, 2, 3):
            sums[name, q, -1].wait_recv()
            total = total + zrecv_[q - 1]
        return total

    for q in range(4):
        rows = pl.ds(q * CLASS, CLASS)
        gd[rows, :] = dot(act[rows, :], og[...], 1, 1)
        begin("d", gd, rd, q)

    @pl.loop(0, 4)
    def _(i):
        rows = pl.ds(pl.multiple_of(lax.div(i, 2) * 512, 512), 512)
        cols = pl.ds(pl.multiple_of(lax.rem(i, 2) * TOK, 128), TOK)
        back = dot(w2[rows, :], og[:, cols], 1, 0)
        slope[rows, cols] = (back * gate[rows, cols]).astype(BF16)

    for q in range(4):
        rows = pl.ds(q * CLASS, CLASS)
        gu[rows, :] = dot(slope[rows, :], nrm[...], 1, 1)
        begin("u", gu, ru, q)

    pown[0] = branch(0)
    core_swap0.wait_recv()
    pown[0] += precv[0]

    advance("d", gd, rd, zd, 3)
    advance("d", gd, rd, zd, 2)
    for i in (2, 3, 4, 5):
        settle(i, moved[i])
    advance("u", gu, ru, zu, 3)
    advance("d", gd, rd, zd, 1)
    advance("u", gu, ru, zu, 2)
    advance("d", gd, rd, zd, 0)

    pair_swap.wait_recv()
    mix[0] = (tok[:, first].astype(F32) + (pown[0] + zrecv[...])).astype(BF16)
    mix_swap = send(mix.at[0], mix.at[1], pair)
    put0 = pltpu.make_async_copy(mix.at[0], mixed_out.at[:, mine], local_sem.at[10])
    put0.start()

    advance("u", gu, ru, zu, 1)
    advance("u", gu, ru, zu, 0)
    down_w_out[...], down_m_out[...], down_v_out[...] = adam_update(
        picked[1], picked[3], picked[5], finish("d", gd, zd)
    )
    up_w_out[...], up_m_out[...], up_v_out[...] = adam_update(
        picked[0], picked[2], picked[4], finish("u", gu, zu)
    )
    mix_swap.wait_recv()
    put1 = pltpu.make_async_copy(mix.at[1], mixed_out.at[:, other], local_sem.at[11])
    put1.start()
    put0.wait()
    put1.wait()
    for copy in started:
        copy.wait_send()


COPIES = 6 + 2 + 6 + 32 + 4 + 38


def local(tokens, out_grad, boundary, up_old, down_old, up_mom, up_var, down_mom, down_var):
    layers = up_old.shape[0]
    hbm = pl.BlockSpec(memory_space=pl.ANY)
    vmem = pl.BlockSpec(memory_space=pltpu.VMEM)
    piece = jax.ShapeDtypeStruct((ROWS, D), F32)
    swap = lambda a: jnp.swapaxes(a, -1, -2)
    V = pltpu.VMEM
    results = pl.pallas_call(
        kernel,
        out_shape=[jax.ShapeDtypeStruct((D, TOK), BF16)] + [piece] * 6,
        in_specs=[pl.BlockSpec(memory_space=pltpu.SMEM)] + [hbm] * 8,
        out_specs=[hbm] + [vmem] * 6,
        scratch_shapes=[
            *[V((layers, 2, ROWS, D), F32)] * 6,
            V((6, ROWS, D), F32),
            V((6, ROWS, D), F32),
            V((6, ROWS, D), F32),
            V((D, TOK), BF16),
            V((D, 2 * TOK), BF16),
            V((D, 2 * TOK), BF16),
            V((UNITS, D), BF16),
            V((UNITS, D), BF16),
            V((UNITS, 2 * TOK), BF16),
            V((UNITS, 2 * TOK), F32),
            V((UNITS, 2 * TOK), BF16),
            V((2, D, HALF_TOK), F32),
            V((2, D, HALF_TOK), F32),
            V((2, D, HALF_TOK), F32),
            V((D, HALF_TOK), F32),
            V((2, D, HALF_TOK), BF16),
            V((UNITS, D), F32),
            V((UNITS, D), F32),
            V((4 * 240, D), F32),
            V((4 * 240, D), F32),
            V((3, ROWS, D), F32),
            V((3, ROWS, D), F32),
            pltpu.SemaphoreType.DMA((12,)),
            pltpu.SemaphoreType.DMA((COPIES,)),
            pltpu.SemaphoreType.DMA((COPIES,)),
        ],
        compiler_params=pltpu.CompilerParams(
            collective_id=0, has_side_effects=True, vmem_limit_bytes=60 * 2**20
        ),
        name="block_step",
    )(
        boundary,
        swap(tokens),
        swap(out_grad),
        swap(up_old),
        down_old,
        swap(up_mom),
        swap(up_var),
        down_mom,
        down_var,
    )
    mixed, up_w, up_m, up_v, down_w, down_m, down_v = results
    return (
        swap(mixed),
        swap(up_w)[None],
        swap(up_m)[None],
        swap(up_v)[None],
        down_w[None],
        down_m[None],
        down_v[None],
    )


def solution(mesh):
    in_specs = (
        P("dp", None),
        P("dp", None),
        P(),
        P("section", None, None, "dp"),
        P("section", None, "dp", None),
        P("section", None, None, "dp"),
        P("section", None, None, "dp"),
        P("section", None, "dp", None),
        P("section", None, "dp", None),
    )
    out_specs = (
        P("dp", None),
        P("section", None, "dp"),
        P("section", None, "dp"),
        P("section", None, "dp"),
        P("section", "dp", None),
        P("section", "dp", None),
        P("section", "dp", None),
    )
    return jax.shard_map(local, mesh=mesh, in_specs=in_specs, out_specs=out_specs, check_vma=False)
```

```python
import functools
import math

import jax
import jax.numpy as jnp
from jax import lax
from jax.experimental import pallas as pl
from jax.experimental.pallas import tpu as pltpu
from jax.sharding import PartitionSpec as P

root_half = 1.0 / math.sqrt(2.0)
root_circle = 1.0 / math.sqrt(2.0 * math.pi)
first_fix = 1.0 - 0.9**10
second_fix = 1.0 - 0.999**10

D = 832
ROWS = 16
TOK = 768
HALF_TOK = TOK // 2
UNITS = 64 * ROWS
CLASS = 8 * ROWS
LATE = UNITS // 2
F32 = jnp.float32
BF16 = jnp.bfloat16


def dot(a, b, ca, cb):
    return lax.dot_general(a, b, (((ca,), (cb,)), ((), ())), preferred_element_type=F32)


def gelu_both(value):
    both = 1.0 + lax.erf(value * root_half)
    return 0.5 * value * both, 0.5 * both + value * jnp.exp(-0.5 * value * value) * root_circle


def layer_norm(tokens):
    wide = tokens.astype(F32)
    center = wide - jnp.mean(wide, axis=0, keepdims=True)
    spread = jnp.mean(center * center, axis=0, keepdims=True)
    return (center * lax.rsqrt(spread + 1e-06)).astype(BF16)


def adam_update(weight, moment, second, grad):
    moment_new = 0.9 * moment + 0.1 * grad
    second_new = 0.999 * second + 0.001 * grad * grad
    stride = moment_new / first_fix / (jnp.sqrt(second_new / second_fix) + 1e-08)
    return (weight - 0.001 * stride, moment_new, second_new)


def flip1(v):
    return v + 1 - 2 * lax.rem(v, 2)


def flip2(v):
    return lax.rem(v + 2, 4)


def flip3(v):
    return 3 - v


def kernel(
    boundary,
    tok_in,
    og_in,
    up_w_in,
    down_w_in,
    up_m_in,
    up_v_in,
    down_m_in,
    down_v_in,
    mixed_out,
    state_out,
    up_w,
    down_w,
    up_m,
    down_m,
    up_v,
    down_v,
    bpiece,
    brecv,
    pick_send,
    pick_recv,
    picked,
    fresh,
    tok,
    nrm,
    og,
    w1,
    w2,
    act,
    gate,
    slope,
    psend,
    pown,
    precv,
    zrecv,
    mix,
    gd,
    gu,
    rd,
    ru,
    zd,
    zu,
    local_sem,
    send_sem,
    recv_sem,
):
    s = lax.axis_index("section")
    d = lax.axis_index("dp")
    x, y, z, c = lax.div(d, 32), lax.rem(lax.div(d, 8), 4), lax.rem(lax.div(d, 2), 4), lax.rem(d, 2)
    core = {"dp": d + 1 - 2 * c}
    pair = {"section": 1 - s}
    xy = (
        {"dp": d + (flip1(x) - x) * 32},
        {"dp": d + (flip3(x) - x) * 32},
        {"dp": d + (flip1(y) - y) * 8},
        {"dp": d + (flip3(y) - y) * 8},
    )
    zs = (
        {"dp": d + (flip1(z) - z) * 2},
        {"dp": d + (flip3(z) - z) * 2},
        {"dp": d + (flip2(z) - z) * 2},
    )
    pair_zs = tuple({"section": 1 - s, "dp": peer["dp"]} for peer in zs)
    state = (up_w, down_w, up_m, down_m, up_v, down_v)
    active = boundary[0]
    slot = lax.rem(active, 6)
    owner = lax.div(active, 6)

    count = [0]
    started = []

    def send(src, dst, dev):
        i = count[0]
        count[0] += 1
        copy = pltpu.make_async_remote_copy(
            src_ref=src,
            dst_ref=dst,
            send_sem=send_sem.at[i],
            recv_sem=recv_sem.at[i],
            device_id=dev,
            device_id_type=pl.DeviceIdType.MESH,
        )
        copy.start()
        started.append(copy)
        return copy

    mine = pl.ds(pl.multiple_of(s * HALF_TOK, 128), HALF_TOK)
    other = pl.ds(pl.multiple_of((1 - s) * HALF_TOK, 128), HALF_TOK)
    first, second = pl.ds(0, HALF_TOK), pl.ds(HALF_TOK, HALF_TOK)

    def fetch(i, src, dst):
        copy = pltpu.make_async_copy(src, dst, local_sem.at[i])
        copy.start()
        return copy

    get_w = [fetch(0, up_w_in, up_w), fetch(1, down_w_in, down_w)]
    barrier = pltpu.get_barrier_semaphore()
    peers = (core, pair) + xy + zs + pair_zs
    for peer in peers:
        pl.semaphore_signal(barrier, inc=1, device_id=peer, device_id_type=pl.DeviceIdType.MESH)
    get_tok = [
        fetch(2, tok_in.at[:, mine], tok.at[:, first]),
        fetch(3, tok_in.at[:, other], tok.at[:, second]),
    ]
    get_og = [
        fetch(4, og_in.at[:, mine], og.at[:, first]),
        fetch(5, og_in.at[:, other], og.at[:, second]),
    ]
    get_mv = [
        fetch(6, up_m_in, up_m),
        fetch(7, down_m_in, down_m),
        fetch(8, up_v_in, up_v),
        fetch(9, down_v_in, down_v),
    ]

    def norm(i):
        at = pl.ds(i * 128, 128)
        nrm[:, at] = layer_norm(tok[:, at])

    for copy in get_w:
        copy.wait()
    for m in (0, 1):
        bpiece[0, m] = state[m][slot, s].astype(BF16)
        bpiece[1, m] = state[m][slot, 1 - s].astype(BF16)
    pl.semaphore_wait(barrier, len(peers))
    offers = [send(bpiece.at[1], brecv.at[0], pair)]
    offers += [send(bpiece.at[0], brecv.at[q], zs[q - 1]) for q in (1, 2, 3)]
    offers += [send(bpiece.at[1], brecv.at[q + 3], pair_zs[q - 1]) for q in (1, 2, 3)]
    for copy in get_og:
        copy.wait()
    og_swap = send(og.at[:, pl.ds(0, TOK)], og.at[:, pl.ds(TOK, TOK)], core)
    for copy in get_tok:
        copy.wait()
    norm(0)
    weights = (w1, w2)
    gathered = {}

    def spread(m, q, j):
        n, at = ROWS << j, q * CLASS
        if j > 0:
            gathered[m, q, j - 1].wait_recv()
        gathered[m, q, j] = send(
            weights[m].at[pl.ds(at, n), :],
            weights[m].at[pl.ds(at + n if j < 3 else LATE + at, n), :],
            xy[(q + j) % 4],
        )

    for q in range(4):
        if q > 0:
            offers[q].wait_recv()
            offers[q + 3].wait_recv()
        else:
            offers[0].wait_recv()
        for m in (0, 1):
            near = bpiece[0, m] if q == 0 else brecv[q, m]
            far = brecv[0, m] if q == 0 else brecv[q + 3, m]
            weights[m][pl.ds(q * CLASS, ROWS), :] = jnp.where(owner == s, near, far)
            spread(m, q, 0)
    norm(1)
    norm(2)
    nrm_swaps = [send(nrm.at[:, first], nrm.at[:, pl.ds(TOK, HALF_TOK)], core)]
    for m in (0, 1):
        for q in range(4):
            spread(m, q, 1)
    norm(3)
    for copy in get_mv:
        copy.wait()
    for i in range(6):
        pick_send[i] = state[i][slot, 1 - s]
    moved = send(pick_send, pick_recv, pair)
    norm(4)
    for m in (0, 1):
        for q in range(4):
            spread(m, q, 2)
    norm(5)
    nrm_swaps.append(send(nrm.at[:, second], nrm.at[:, pl.ds(TOK + HALF_TOK, HALF_TOK)], core))
    for q in range(4):
        spread(0, q, 3)

    def forward(part, t):
        rows, cols = pl.ds(part * LATE, LATE), pl.ds(t * TOK, TOK)
        value, rate = gelu_both(dot(w1[rows, :], nrm[:, cols], 1, 0))
        act[rows, cols] = value.astype(BF16)
        gate[rows, cols] = rate

    def backward(part):
        @pl.loop(0, 2)
        def _(t):
            rows, cols = pl.ds(part * LATE, LATE), pl.ds(pl.multiple_of(t * TOK, 128), TOK)
            back = dot(w2[rows, :], og[:, cols], 1, 0)
            slope[rows, cols] = (back * gate[rows, cols]).astype(BF16)

    def branch(block):
        return dot(w2[...], act[:, pl.ds(block * HALF_TOK, HALF_TOK)], 0, 0)

    forward(0, 0)
    for copy in nrm_swaps:
        copy.wait_recv()
    forward(0, 1)
    for q in range(4):
        gathered[0, q, 3].wait_recv()
    for q in range(4):
        spread(1, q, 3)
    forward(1, 0)
    forward(1, 1)

    sums = {}
    early, late = pl.ds(0, LATE), pl.ds(LATE, LATE)

    def begin(name, grad, recv):
        for q in range(4):
            sums[name, q, 3] = send(
                grad.at[pl.ds(LATE + q * CLASS, CLASS), :],
                recv.at[pl.ds(q * 240, CLASS), :],
                xy[(q + 3) % 4],
            )

    def advance(name, grad, recv, zrecv_, j):
        n = ROWS << j
        at = (16 - (2 << j)) * ROWS
        for q in range(4):
            base, low = q * CLASS, q * 240 + at
            sums[name, q, j].wait_recv()
            if j > 0:
                h = n // 2
                grad[pl.ds(base + h, h), :] += recv[pl.ds(low + h, h), :]
                sums[name, q, j - 1] = send(
                    grad.at[pl.ds(base + h, h), :],
                    recv.at[pl.ds(low + n, h), :],
                    xy[(q + j - 1) % 4],
                )
                grad[pl.ds(base, h), :] += recv[pl.ds(low, h), :]
            else:
                grad[pl.ds(base, n), :] += recv[pl.ds(low, n), :]
                if q > 0:
                    sums[name, q, -1] = send(grad.at[pl.ds(base, n), :], zrecv_.at[q - 1], zs[q - 1])

    def finish(name, grad, zrecv_):
        total = grad[pl.ds(0, ROWS), :]
        for q in (1, 2, 3):
            sums[name, q, -1].wait_recv()
            total = total + zrecv_[q - 1]
        return total

    og_swap.wait_recv()
    gd[late, :] = dot(act[late, :], og[...], 1, 1)
    begin("d", gd, rd)
    for q in range(4):
        gathered[1, q, 3].wait_recv()

    psend[1] = branch(3)
    core_swap1 = send(psend.at[1], precv.at[1], core)
    pown[1] = branch(1)
    gd[early, :] = dot(act[early, :], og[...], 1, 1)
    core_swap1.wait_recv()
    pown[1] += precv[1]
    pair_swap = send(pown.at[1], zrecv, pair)
    backward(1)
    gu[late, :] = dot(slope[late, :], nrm[...], 1, 1)
    begin("u", gu, ru)
    psend[0] = branch(2)
    core_swap0 = send(psend.at[0], precv.at[0], core)
    pown[0] = branch(0)
    advance("d", gd, rd, zd, 3)
    backward(0)
    gu[early, :] = dot(slope[early, :], nrm[...], 1, 1)
    core_swap0.wait_recv()
    pown[0] += precv[0]
    advance("d", gd, rd, zd, 2)
    advance("u", gu, ru, zu, 3)
    advance("d", gd, rd, zd, 1)
    advance("u", gu, ru, zu, 2)
    moved.wait_recv()
    for i in range(6):
        picked[i] = jnp.where(owner == s, state[i][slot, s], pick_recv[i])
    advance("d", gd, rd, zd, 0)
    advance("u", gu, ru, zu, 1)

    pair_swap.wait_recv()
    mix[0] = (tok[:, first].astype(F32) + (pown[0] + zrecv[...])).astype(BF16)
    mix_swap = send(mix.at[0], mix.at[1], pair)
    puts = [pltpu.make_async_copy(mix.at[0], mixed_out.at[:, mine], local_sem.at[10])]
    puts[0].start()
    advance("u", gu, ru, zu, 0)
    fresh[3], fresh[4], fresh[5] = adam_update(picked[1], picked[3], picked[5], finish("d", gd, zd))
    fresh[0], fresh[1], fresh[2] = adam_update(picked[0], picked[2], picked[4], finish("u", gu, zu))
    puts.append(pltpu.make_async_copy(fresh, state_out, local_sem.at[12]))
    puts[1].start()
    mix_swap.wait_recv()
    puts.append(pltpu.make_async_copy(mix.at[1], mixed_out.at[:, other], local_sem.at[11]))
    puts[2].start()
    for copy in puts:
        copy.wait()
    for copy in started:
        copy.wait_send()


COPIES = 7 + 1 + 2 + 1 + 32 + 4 + 38


def hand_out(mixed_in, state_in, mixed_out, *rest):
    outs, sem = rest[:6], rest[6]
    copies = [pltpu.make_async_copy(mixed_in, mixed_out, sem.at[6])]
    copies += [pltpu.make_async_copy(state_in.at[i], outs[i], sem.at[i]) for i in range(6)]
    for copy in copies:
        copy.start()
    for copy in copies:
        copy.wait()


def local(tokens, out_grad, boundary, up_old, down_old, up_mom, up_var, down_mom, down_var):
    layers = up_old.shape[0]
    hbm = pl.BlockSpec(memory_space=pl.ANY)
    swap = lambda a: jnp.swapaxes(a, -1, -2)
    V = pltpu.VMEM
    mixed_type = jax.ShapeDtypeStruct((D, TOK), BF16)
    results = pl.pallas_call(
        kernel,
        out_shape=[mixed_type, jax.ShapeDtypeStruct((6, ROWS, D), F32)],
        in_specs=[pl.BlockSpec(memory_space=pltpu.SMEM)] + [hbm] * 8,
        out_specs=[hbm] * 2,
        scratch_shapes=[
            *[V((layers, 2, ROWS, D), F32)] * 6,
            V((2, 2, ROWS, D), BF16),
            V((7, 2, ROWS, D), BF16),
            V((6, ROWS, D), F32),
            V((6, ROWS, D), F32),
            V((6, ROWS, D), F32),
            V((6, ROWS, D), F32),
            V((D, TOK), BF16),
            V((D, 2 * TOK), BF16),
            V((D, 2 * TOK), BF16),
            V((UNITS, D), BF16),
            V((UNITS, D), BF16),
            V((UNITS, 2 * TOK), BF16),
            V((UNITS, 2 * TOK), F32),
            V((UNITS, 2 * TOK), BF16),
            V((2, D, HALF_TOK), F32),
            V((2, D, HALF_TOK), F32),
            V((2, D, HALF_TOK), F32),
            V((D, HALF_TOK), F32),
            V((2, D, HALF_TOK), BF16),
            V((UNITS, D), F32),
            V((UNITS, D), F32),
            V((4 * 240, D), F32),
            V((4 * 240, D), F32),
            V((3, ROWS, D), F32),
            V((3, ROWS, D), F32),
            pltpu.SemaphoreType.DMA((13,)),
            pltpu.SemaphoreType.DMA((COPIES,)),
            pltpu.SemaphoreType.DMA((COPIES,)),
        ],
        compiler_params=pltpu.CompilerParams(
            collective_id=0, has_side_effects=True, vmem_limit_bytes=60 * 2**20
        ),
        name="block_step",
    )(
        boundary,
        swap(tokens),
        swap(out_grad),
        swap(up_old),
        down_old,
        swap(up_mom),
        swap(up_var),
        down_mom,
        down_var,
    )
    mixed, up_w, up_m, up_v, down_w, down_m, down_v = pl.pallas_call(
        hand_out,
        out_shape=[mixed_type] + [jax.ShapeDtypeStruct((ROWS, D), F32)] * 6,
        in_specs=[hbm] * 2,
        out_specs=[hbm] * 7,
        scratch_shapes=[pltpu.SemaphoreType.DMA((7,))],
        compiler_params=pltpu.CompilerParams(vmem_limit_bytes=60 * 2**20),
        name="hand_out",
    )(*results)
    return (
        swap(mixed),
        swap(up_w)[None],
        swap(up_m)[None],
        swap(up_v)[None],
        down_w[None],
        down_m[None],
        down_v[None],
    )


def solution(mesh):
    in_specs = (
        P("dp", None),
        P("dp", None),
        P(),
        P("section", None, None, "dp"),
        P("section", None, "dp", None),
        P("section", None, None, "dp"),
        P("section", None, None, "dp"),
        P("section", None, "dp", None),
        P("section", None, "dp", None),
    )
    out_specs = (
        P("dp", None),
        P("section", None, "dp"),
        P("section", None, "dp"),
        P("section", None, "dp"),
        P("section", "dp", None),
        P("section", "dp", None),
        P("section", "dp", None),
    )
    return jax.shard_map(local, mesh=mesh, in_specs=in_specs, out_specs=out_specs, check_vma=False)
```

```python
import functools
import math

import jax
import jax.numpy as jnp
from jax import lax
from jax.experimental import pallas as pl
from jax.experimental.pallas import tpu as pltpu
from jax.sharding import PartitionSpec as P

root_half = 1.0 / math.sqrt(2.0)
root_circle = 1.0 / math.sqrt(2.0 * math.pi)
first_fix = 1.0 - 0.9**10
second_fix = 1.0 - 0.999**10

D = 832
ROWS = 16
TOK = 768
HALF_TOK = TOK // 2
UNITS = 64 * ROWS
CLASS = 8 * ROWS
LATE = UNITS // 2
F32 = jnp.float32
BF16 = jnp.bfloat16


def dot(a, b, ca, cb):
    return lax.dot_general(a, b, (((ca,), (cb,)), ((), ())), preferred_element_type=F32)


def gelu_both(value):
    both = 1.0 + lax.erf(value * root_half)
    return 0.5 * value * both, 0.5 * both + value * jnp.exp(-0.5 * value * value) * root_circle


def layer_norm(tokens):
    wide = tokens.astype(F32)
    center = wide - jnp.mean(wide, axis=0, keepdims=True)
    spread = jnp.mean(center * center, axis=0, keepdims=True)
    return (center * lax.rsqrt(spread + 1e-06)).astype(BF16)


def adam_update(weight, moment, second, grad):
    moment_new = 0.9 * moment + 0.1 * grad
    second_new = 0.999 * second + 0.001 * grad * grad
    stride = moment_new / first_fix / (jnp.sqrt(second_new / second_fix) + 1e-08)
    return (weight - 0.001 * stride, moment_new, second_new)


def tiles(width):
    return [pl.ds(at, min(128, width - at)) for at in range(0, width, 128)]


def encode(x, code, scale):
    n, w = x.shape
    top = jnp.max(jnp.abs(x).reshape(n // 8, 8, w), axis=0)
    best = top[:, :128]
    for at in range(128, w - 127, 128):
        best = jnp.maximum(best, top[:, at : at + 128])
    rest = w % 128
    if rest:
        best = jnp.concatenate([jnp.maximum(best[:, :rest], top[:, w - rest :]), best[:, rest:]], axis=1)
    unit = jnp.maximum(best, 1e-30) * (1.0 / 32760.0)
    scale[...] = unit
    per = 1.0 / unit
    for cols in tiles(w):
        part = x[:, cols.start : cols.start + cols.size].reshape(n // 8, 8, cols.size)
        part = jnp.round(part * per[None, :, : cols.size])
        code[:, cols] = part.astype(jnp.int32).astype(jnp.int16).reshape(n, cols.size)


def decode(code, scale, cols):
    part = code[:, cols].astype(jnp.int32).astype(F32)
    n, w = part.shape
    return (part.reshape(n // 8, 8, w) * scale[:, pl.ds(0, w)][None]).reshape(n, w)


def decode_wide(code, scale):
    return jnp.concatenate([decode(code, scale, cols) for cols in tiles(code.shape[1])], axis=1)


def flip1(v):
    return v + 1 - 2 * lax.rem(v, 2)


def flip2(v):
    return lax.rem(v + 2, 4)


def flip3(v):
    return 3 - v


def kernel(
    boundary,
    tok_in,
    og_in,
    up_w_in,
    down_w_in,
    up_m_in,
    up_v_in,
    down_m_in,
    down_v_in,
    mixed_out,
    state_out,
    up_w,
    down_w,
    up_m,
    down_m,
    up_v,
    down_v,
    bpiece,
    brecv,
    pick_send,
    pick_recv,
    picked,
    fresh,
    tok,
    nrm,
    og,
    w1,
    w2,
    act,
    gate,
    slope,
    psend,
    pown,
    precv,
    pair_code,
    pair_scale,
    pair_code_in,
    pair_scale_in,
    mix,
    gd,
    gu,
    sum_code,
    sum_scale,
    sum_code_in,
    sum_scale_in,
    local_sem,
    send_sem,
    recv_sem,
):
    s = lax.axis_index("section")
    d = lax.axis_index("dp")
    x, y, z, c = lax.div(d, 32), lax.rem(lax.div(d, 8), 4), lax.rem(lax.div(d, 2), 4), lax.rem(d, 2)
    core = {"dp": d + 1 - 2 * c}
    pair = {"section": 1 - s}
    xy = (
        {"dp": d + (flip1(x) - x) * 32},
        {"dp": d + (flip3(x) - x) * 32},
        {"dp": d + (flip1(y) - y) * 8},
        {"dp": d + (flip3(y) - y) * 8},
    )
    zs = (
        {"dp": d + (flip1(z) - z) * 2},
        {"dp": d + (flip3(z) - z) * 2},
        {"dp": d + (flip2(z) - z) * 2},
    )
    state = (up_w, down_w, up_m, down_m, up_v, down_v)
    active = boundary[0]
    slot = lax.rem(active, 6)
    owner = lax.div(active, 6)

    count = [0]
    started = []

    def send(src, dst, dev):
        i = count[0]
        count[0] += 1
        copy = pltpu.make_async_remote_copy(
            src_ref=src,
            dst_ref=dst,
            send_sem=send_sem.at[i],
            recv_sem=recv_sem.at[i],
            device_id=dev,
            device_id_type=pl.DeviceIdType.MESH,
        )
        copy.start()
        started.append(copy)
        return copy

    mine = pl.ds(pl.multiple_of(s * HALF_TOK, 128), HALF_TOK)
    other = pl.ds(pl.multiple_of((1 - s) * HALF_TOK, 128), HALF_TOK)
    first, second = pl.ds(0, HALF_TOK), pl.ds(HALF_TOK, HALF_TOK)

    def fetch(i, src, dst):
        copy = pltpu.make_async_copy(src, dst, local_sem.at[i])
        copy.start()
        return copy

    get_w = [fetch(0, up_w_in, up_w), fetch(1, down_w_in, down_w)]
    barrier = pltpu.get_barrier_semaphore()
    peers = (core, pair) + xy + zs
    for peer in peers:
        pl.semaphore_signal(barrier, inc=1, device_id=peer, device_id_type=pl.DeviceIdType.MESH)
    get_tok = [
        fetch(2, tok_in.at[:, mine], tok.at[:, first]),
        fetch(3, tok_in.at[:, other], tok.at[:, second]),
    ]
    get_og = [
        fetch(4, og_in.at[:, mine], og.at[:, first]),
        fetch(5, og_in.at[:, other], og.at[:, second]),
    ]
    get_mv = [
        fetch(6, up_m_in, up_m),
        fetch(7, down_m_in, down_m),
        fetch(8, up_v_in, up_v),
        fetch(9, down_v_in, down_v),
    ]

    def norm(i):
        at = pl.ds(i * 128, 128)
        nrm[:, at] = layer_norm(tok[:, at])

    for copy in get_w:
        copy.wait()
    for m in (0, 1):
        bpiece[0, m] = state[m][slot, s].astype(BF16)
        bpiece[1, m] = state[m][slot, 1 - s].astype(BF16)
    pl.semaphore_wait(barrier, len(peers))
    offers = [send(bpiece.at[1, m], brecv.at[m], pair) for m in (0, 1)]
    for copy in get_tok:
        copy.wait()
    weights = (w1, w2)
    gathered = {}

    def spread(m, q, j):
        n, at = ROWS << j, q * CLASS
        if j > 0 or q > 0:
            gathered[m, q, j - 1].wait_recv()
        gathered[m, q, j] = send(
            weights[m].at[pl.ds(at, n), :],
            weights[m].at[pl.ds(at + n if j < 3 else LATE + at, n), :],
            xy[(q + j) % 4],
        )

    for m in (0, 1):
        offers[m].wait_recv()
        weights[m][pl.ds(0, ROWS), :] = jnp.where(owner == s, bpiece[0, m], brecv[m])
        for q in (1, 2, 3):
            gathered[m, q, -1] = send(
                weights[m].at[pl.ds(0, ROWS), :], weights[m].at[pl.ds(q * CLASS, ROWS), :], zs[q - 1]
            )
        spread(m, 0, 0)
    for copy in get_og:
        copy.wait()
    og_swap = send(og.at[:, pl.ds(0, TOK)], og.at[:, pl.ds(TOK, TOK)], core)
    norm(0)
    for m in (0, 1):
        for q in (1, 2, 3):
            spread(m, q, 0)
    norm(1)
    norm(2)
    nrm_swaps = [send(nrm.at[:, first], nrm.at[:, pl.ds(TOK, HALF_TOK)], core)]
    for m in (0, 1):
        for q in range(4):
            spread(m, q, 1)
    norm(3)
    for copy in get_mv:
        copy.wait()
    for i in range(6):
        pick_send[i] = state[i][slot, 1 - s]
    moved = send(pick_send, pick_recv, pair)
    norm(4)
    for m in (0, 1):
        for q in range(4):
            spread(m, q, 2)
    norm(5)
    nrm_swaps.append(send(nrm.at[:, second], nrm.at[:, pl.ds(TOK + HALF_TOK, HALF_TOK)], core))
    for q in range(4):
        spread(0, q, 3)

    def forward(part, t):
        rows, cols = pl.ds(part * LATE, LATE), pl.ds(t * TOK, TOK)
        value, rate = gelu_both(dot(w1[rows, :], nrm[:, cols], 1, 0))
        act[rows, cols] = value.astype(BF16)
        gate[rows, cols] = rate

    def backward(part):
        @pl.loop(0, 2)
        def _(t):
            rows, cols = pl.ds(part * LATE, LATE), pl.ds(pl.multiple_of(t * TOK, 128), TOK)
            back = dot(w2[rows, :], og[:, cols], 1, 0)
            slope[rows, cols] = (back * gate[rows, cols]).astype(BF16)

    def branch(block):
        return dot(w2[...], act[:, pl.ds(block * HALF_TOK, HALF_TOK)], 0, 0)

    forward(0, 0)
    for copy in nrm_swaps:
        copy.wait_recv()
    forward(0, 1)
    for q in range(4):
        gathered[0, q, 3].wait_recv()
    for q in range(4):
        spread(1, q, 3)
    forward(1, 0)
    forward(1, 1)

    sums = {}
    grads = (gd, gu)
    early, late = pl.ds(0, LATE), pl.ds(LATE, LATE)

    def rows_of(j, q):
        return pl.ds(q * 256 + (240 if j < 0 else (16 - (2 << j)) * ROWS), ROWS if j < 0 else ROWS << j)

    def ship(g, q, j, value):
        rows, k = rows_of(j, q), 5 * q + j + 1
        to = xy[(q + j) % 4] if j >= 0 else zs[q - 1]
        encode(value, sum_code.at[g, rows, :], sum_scale.at[g, k])
        sums[g, q, j] = (
            send(sum_code.at[g, rows, :], sum_code_in.at[g, rows, :], to),
            send(sum_scale.at[g, k], sum_scale_in.at[g, k], to),
        )

    def arrived(g, q, j):
        for copy in sums[g, q, j]:
            copy.wait_recv()
        return decode_wide(sum_code_in.at[g, rows_of(j, q), :], sum_scale_in.at[g, 5 * q + j + 1])

    def begin(g):
        for q in range(4):
            ship(g, q, 3, grads[g][pl.ds(LATE + q * CLASS, CLASS), :])

    def advance(g, j):
        n = ROWS << j
        for q in range(4):
            rows = pl.ds(q * CLASS, n)
            value = grads[g][rows, :] + arrived(g, q, j)
            if j > 0:
                ship(g, q, j - 1, value[n // 2 :])
                grads[g][pl.ds(q * CLASS, n // 2), :] = value[: n // 2]
            elif q > 0:
                ship(g, q, -1, value)
            else:
                grads[g][rows, :] = value

    def finish(g):
        total = grads[g][pl.ds(0, ROWS), :]
        for q in (1, 2, 3):
            total = total + arrived(g, q, -1)
        return total

    og_swap.wait_recv()
    gd[late, :] = dot(act[late, :], og[...], 1, 1)
    begin(0)
    for q in range(4):
        gathered[1, q, 3].wait_recv()

    pair_swaps = {}

    def exchange(b):
        core_swaps[b].wait_recv()
        for i, cols in enumerate(tiles(HALF_TOK)):
            value = pown[b, :, cols] + precv[b, :, cols]
            encode(value, pair_code.at[b, :, cols], pair_scale.at[b, :, cols])
        pair_swaps[b] = (
            send(pair_code.at[b], pair_code_in.at[1 - b], pair),
            send(pair_scale.at[b], pair_scale_in.at[1 - b], pair),
        )

    def complete(b, where, sem):
        for copy in pair_swaps[1 - b]:
            copy.wait_recv()
        for cols in tiles(HALF_TOK):
            at = pl.ds(b * HALF_TOK + cols.start, 128)
            near = decode(pair_code.at[b, :, cols], pair_scale.at[b, :, cols], pl.ds(0, 128))
            far = decode(pair_code_in.at[b, :, cols], pair_scale_in.at[b, :, cols], pl.ds(0, 128))
            mix[b, :, cols] = (tok[:, at].astype(F32) + (near + far)).astype(BF16)
        put = pltpu.make_async_copy(mix.at[b], mixed_out.at[:, where], local_sem.at[sem])
        put.start()
        return put

    core_swaps = {}
    psend[1] = branch(3)
    core_swaps[1] = send(psend.at[1], precv.at[1], core)
    pown[1] = branch(1)
    exchange(1)
    psend[0] = branch(2)
    core_swaps[0] = send(psend.at[0], precv.at[0], core)
    gd[early, :] = dot(act[early, :], og[...], 1, 1)
    pown[0] = branch(0)
    exchange(0)
    advance(0, 3)
    backward(1)
    gu[late, :] = dot(slope[late, :], nrm[...], 1, 1)
    begin(1)
    advance(0, 2)
    backward(0)
    gu[early, :] = dot(slope[early, :], nrm[...], 1, 1)
    advance(0, 1)
    advance(1, 3)
    advance(0, 0)
    advance(1, 2)
    moved.wait_recv()
    for i in range(6):
        picked[i] = jnp.where(owner == s, state[i][slot, s], pick_recv[i])
    advance(1, 1)
    puts = [complete(0, mine, 11)]
    advance(1, 0)
    fresh[3], fresh[4], fresh[5] = adam_update(picked[1], picked[3], picked[5], finish(0))
    fresh[0], fresh[1], fresh[2] = adam_update(picked[0], picked[2], picked[4], finish(1))
    puts.append(pltpu.make_async_copy(fresh, state_out, local_sem.at[12]))
    puts[1].start()
    puts.append(complete(1, other, 10))
    for copy in puts:
        copy.wait()
    for copy in started:
        copy.wait_send()


COPIES = 2 + 6 + 1 + 2 + 1 + 32 + 2 + 4 + 2 * 38


def hand_out(mixed_in, state_in, mixed_out, *rest):
    outs, (mixed, state, sem) = rest[:6], rest[6:]
    bands = [pl.ds(i * D // 4, D // 4) for i in range(4)]
    gets = [pltpu.make_async_copy(mixed_in.at[band, :], mixed.at[band, :], sem.at[i]) for i, band in enumerate(bands)]
    gets.append(pltpu.make_async_copy(state_in, state, sem.at[4]))
    puts = [[pltpu.make_async_copy(mixed.at[band, :], mixed_out.at[band, :], sem.at[5 + i])] for i, band in enumerate(bands)]
    puts.append([pltpu.make_async_copy(state.at[i], outs[i], sem.at[9 + i]) for i in range(6)])
    for get in gets:
        get.start()
    for get, put in zip(gets, puts):
        get.wait()
        for copy in put:
            copy.start()
    for put in puts:
        for copy in put:
            copy.wait()


def local(tokens, out_grad, boundary, up_old, down_old, up_mom, up_var, down_mom, down_var):
    layers = up_old.shape[0]
    hbm = pl.BlockSpec(memory_space=pl.ANY)
    swap = lambda a: jnp.swapaxes(a, -1, -2)
    V = pltpu.VMEM
    mixed_type = jax.ShapeDtypeStruct((D, TOK), BF16)
    results = pl.pallas_call(
        kernel,
        out_shape=[mixed_type, jax.ShapeDtypeStruct((6, ROWS, D), F32)],
        in_specs=[pl.BlockSpec(memory_space=pltpu.SMEM)] + [hbm] * 8,
        out_specs=[hbm] * 2,
        scratch_shapes=[
            *[V((layers, 2, ROWS, D), F32)] * 6,
            V((2, 2, ROWS, D), BF16),
            V((2, ROWS, D), BF16),
            V((6, ROWS, D), F32),
            V((6, ROWS, D), F32),
            V((6, ROWS, D), F32),
            V((6, ROWS, D), F32),
            V((D, TOK), BF16),
            V((D, 2 * TOK), BF16),
            V((D, 2 * TOK), BF16),
            V((UNITS, D), BF16),
            V((UNITS, D), BF16),
            V((UNITS, 2 * TOK), BF16),
            V((UNITS, 2 * TOK), F32),
            V((UNITS, 2 * TOK), BF16),
            V((2, D, HALF_TOK), F32),
            V((2, D, HALF_TOK), F32),
            V((2, D, HALF_TOK), F32),
            *[V((2, D, HALF_TOK), jnp.int16), V((2, 8, HALF_TOK), F32)] * 2,
            V((2, D, HALF_TOK), BF16),
            V((UNITS, D), F32),
            V((UNITS, D), F32),
            *[V((2, 4 * 256, D), jnp.int16), V((2, 20, 8, 128), F32)] * 2,
            pltpu.SemaphoreType.DMA((13,)),
            pltpu.SemaphoreType.DMA((COPIES,)),
            pltpu.SemaphoreType.DMA((COPIES,)),
        ],
        compiler_params=pltpu.CompilerParams(
            collective_id=0, has_side_effects=True, vmem_limit_bytes=60 * 2**20
        ),
        name="block_step",
    )(
        boundary,
        swap(tokens),
        swap(out_grad),
        swap(up_old),
        down_old,
        swap(up_mom),
        swap(up_var),
        down_mom,
        down_var,
    )
    mixed, up_w, up_m, up_v, down_w, down_m, down_v = pl.pallas_call(
        hand_out,
        out_shape=[mixed_type] + [jax.ShapeDtypeStruct((ROWS, D), F32)] * 6,
        in_specs=[hbm] * 2,
        out_specs=[hbm] * 7,
        scratch_shapes=[V((D, TOK), BF16), V((6, ROWS, D), F32), pltpu.SemaphoreType.DMA((15,))],
        compiler_params=pltpu.CompilerParams(vmem_limit_bytes=60 * 2**20),
        name="hand_out",
    )(*results)
    return (
        swap(mixed),
        swap(up_w)[None],
        swap(up_m)[None],
        swap(up_v)[None],
        down_w[None],
        down_m[None],
        down_v[None],
    )


def solution(mesh):
    in_specs = (
        P("dp", None),
        P("dp", None),
        P(),
        P("section", None, None, "dp"),
        P("section", None, "dp", None),
        P("section", None, None, "dp"),
        P("section", None, None, "dp"),
        P("section", None, "dp", None),
        P("section", None, "dp", None),
    )
    out_specs = (
        P("dp", None),
        P("section", None, "dp"),
        P("section", None, "dp"),
        P("section", None, "dp"),
        P("section", "dp", None),
        P("section", "dp", None),
        P("section", "dp", None),
    )
    return jax.shard_map(local, mesh=mesh, in_specs=in_specs, out_specs=out_specs, check_vma=False)
```

```python
import functools
import math

import jax
import jax.numpy as jnp
from jax import lax
from jax.experimental import pallas as pl
from jax.experimental.pallas import tpu as pltpu
from jax.sharding import PartitionSpec as P

root_half = 1.0 / math.sqrt(2.0)
root_circle = 1.0 / math.sqrt(2.0 * math.pi)
first_fix = 1.0 - 0.9**10
second_fix = 1.0 - 0.999**10

D = 832
ROWS = 16
TOK = 768
HALF_TOK = TOK // 2
UNITS = 64 * ROWS
CLASS = 8 * ROWS
LATE = UNITS // 2
F32 = jnp.float32
BF16 = jnp.bfloat16


def dot(a, b, ca, cb):
    return lax.dot_general(a, b, (((ca,), (cb,)), ((), ())), preferred_element_type=F32)


def gelu_both(value):
    both = 1.0 + lax.erf(value * root_half)
    return 0.5 * value * both, 0.5 * both + value * jnp.exp(-0.5 * value * value) * root_circle


def layer_norm(tokens):
    wide = tokens.astype(F32)
    center = wide - jnp.mean(wide, axis=0, keepdims=True)
    spread = jnp.mean(center * center, axis=0, keepdims=True)
    return (center * lax.rsqrt(spread + 1e-06)).astype(BF16)


def adam_update(weight, moment, second, grad):
    moment_new = 0.9 * moment + 0.1 * grad
    second_new = 0.999 * second + 0.001 * grad * grad
    stride = moment_new / first_fix / (jnp.sqrt(second_new / second_fix) + 1e-08)
    return (weight - 0.001 * stride, moment_new, second_new)


def tiles(width):
    return [pl.ds(at, min(128, width - at)) for at in range(0, width, 128)]


def encode(x, code, scale):
    n, w = x.shape
    top = jnp.max(jnp.abs(x).reshape(n // 8, 8, w), axis=0)
    best = top[:, :128]
    for at in range(128, w - 127, 128):
        best = jnp.maximum(best, top[:, at : at + 128])
    rest = w % 128
    if rest:
        best = jnp.concatenate([jnp.maximum(best[:, :rest], top[:, w - rest :]), best[:, rest:]], axis=1)
    unit = jnp.maximum(best, 1e-30) * (1.0 / 32760.0)
    scale[...] = unit
    per = 1.0 / unit
    for cols in tiles(w):
        part = x[:, cols.start : cols.start + cols.size].reshape(n // 8, 8, cols.size)
        part = jnp.round(part * per[None, :, : cols.size])
        code[:, cols] = part.astype(jnp.int32).astype(jnp.int16).reshape(n, cols.size)


def decode(code, scale, cols):
    part = code[:, cols].astype(jnp.int32).astype(F32)
    n, w = part.shape
    return (part.reshape(n // 8, 8, w) * scale[:, pl.ds(0, w)][None]).reshape(n, w)


def decode_wide(code, scale):
    return jnp.concatenate([decode(code, scale, cols) for cols in tiles(code.shape[1])], axis=1)


def flip1(v):
    return v + 1 - 2 * lax.rem(v, 2)


def flip2(v):
    return lax.rem(v + 2, 4)


def flip3(v):
    return 3 - v


def kernel(
    boundary,
    tok_in,
    og_in,
    up_w_in,
    down_w_in,
    up_m_in,
    up_v_in,
    down_m_in,
    down_v_in,
    mixed_out,
    state_out,
    up_w,
    down_w,
    up_m,
    down_m,
    up_v,
    down_v,
    bpiece,
    brecv,
    pick_send,
    pick_recv,
    picked,
    fresh,
    tok,
    nrm,
    og,
    w1,
    w2,
    act,
    gate,
    slope,
    psend,
    pown,
    precv,
    pair_code,
    pair_scale,
    pair_code_in,
    pair_scale_in,
    mix,
    gd,
    gu,
    sum_code,
    sum_scale,
    sum_code_in,
    sum_scale_in,
    local_sem,
    send_sem,
    recv_sem,
):
    s = lax.axis_index("section")
    d = lax.axis_index("dp")
    x, y, z, c = lax.div(d, 32), lax.rem(lax.div(d, 8), 4), lax.rem(lax.div(d, 2), 4), lax.rem(d, 2)
    core = {"dp": d + 1 - 2 * c}
    pair = {"section": 1 - s}
    xy = (
        {"dp": d + (flip1(x) - x) * 32},
        {"dp": d + (flip3(x) - x) * 32},
        {"dp": d + (flip1(y) - y) * 8},
        {"dp": d + (flip3(y) - y) * 8},
    )
    zs = (
        {"dp": d + (flip1(z) - z) * 2},
        {"dp": d + (flip3(z) - z) * 2},
        {"dp": d + (flip2(z) - z) * 2},
    )
    state = (up_w, down_w, up_m, down_m, up_v, down_v)
    active = boundary[0]
    slot = lax.rem(active, 6)
    owner = lax.div(active, 6)

    count = [0]
    started = []

    def send(src, dst, dev):
        i = count[0]
        count[0] += 1
        copy = pltpu.make_async_remote_copy(
            src_ref=src,
            dst_ref=dst,
            send_sem=send_sem.at[i],
            recv_sem=recv_sem.at[i],
            device_id=dev,
            device_id_type=pl.DeviceIdType.MESH,
        )
        copy.start()
        started.append(copy)
        return copy

    mine = pl.ds(pl.multiple_of(s * HALF_TOK, 128), HALF_TOK)
    other = pl.ds(pl.multiple_of((1 - s) * HALF_TOK, 128), HALF_TOK)
    first, second = pl.ds(0, HALF_TOK), pl.ds(HALF_TOK, HALF_TOK)

    def fetch(i, src, dst):
        copy = pltpu.make_async_copy(src, dst, local_sem.at[i])
        copy.start()
        return copy

    get_w = [fetch(0, up_w_in, up_w), fetch(1, down_w_in, down_w)]
    barrier = pltpu.get_barrier_semaphore()
    peers = (core, pair) + xy + zs
    for peer in peers:
        pl.semaphore_signal(barrier, inc=1, device_id=peer, device_id_type=pl.DeviceIdType.MESH)
    get_tok = [
        fetch(2, tok_in.at[:, mine], tok.at[:, first]),
        fetch(3, tok_in.at[:, other], tok.at[:, second]),
    ]
    get_og = [
        fetch(4, og_in.at[:, mine], og.at[:, first]),
        fetch(5, og_in.at[:, other], og.at[:, second]),
    ]
    get_mv = [
        fetch(6, up_m_in, up_m),
        fetch(7, down_m_in, down_m),
        fetch(8, up_v_in, up_v),
        fetch(9, down_v_in, down_v),
    ]

    def norm(i):
        at = pl.ds(i * 128, 128)
        nrm[:, at] = layer_norm(tok[:, at])

    for copy in get_w:
        copy.wait()
    for m in (0, 1):
        bpiece[0, m] = state[m][slot, s].astype(BF16)
        bpiece[1, m] = state[m][slot, 1 - s].astype(BF16)
    pl.semaphore_wait(barrier, len(peers))
    offers = [send(bpiece.at[1, m], brecv.at[m], pair) for m in (0, 1)]
    for copy in get_tok:
        copy.wait()
    weights = (w1, w2)
    gathered = {}
    arrivals = {}

    def row_of(q, slot_):
        return q * CLASS + (slot_ * ROWS if slot_ < 8 else LATE + (slot_ - 8) * ROWS)

    def spread(m, q, j):
        if j == 0:
            if q > 0:
                gathered[m, q, -1].wait_recv()
            low, size = 0, 1
        else:
            low = size = 1 << (j - 1)
            for copy in arrivals[m, q, j - 1]:
                copy.wait_recv()
        for k in range(j, 4):
            copy = send(
                weights[m].at[pl.ds(row_of(q, low), size * ROWS), :],
                weights[m].at[pl.ds(row_of(q, (1 << k) + low), size * ROWS), :],
                xy[(q + k) % 4],
            )
            arrivals.setdefault((m, q, k), []).append(copy)

    def spread_all(m, j):
        for q in range(4):
            spread(m, q, j)

    def all_here(m, j):
        for q in range(4):
            for copy in arrivals[m, q, j]:
                copy.wait_recv()

    for m in (0, 1):
        offers[m].wait_recv()
        weights[m][pl.ds(0, ROWS), :] = jnp.where(owner == s, bpiece[0, m], brecv[m])
        for q in (1, 2, 3):
            gathered[m, q, -1] = send(
                weights[m].at[pl.ds(0, ROWS), :], weights[m].at[pl.ds(q * CLASS, ROWS), :], zs[q - 1]
            )
    for copy in get_og:
        copy.wait()
    og_swap = send(og.at[:, pl.ds(0, TOK)], og.at[:, pl.ds(TOK, TOK)], core)
    norm(0)
    spread_all(0, 0)
    norm(1)
    spread_all(0, 1)
    norm(2)
    nrm_swaps = [send(nrm.at[:, first], nrm.at[:, pl.ds(TOK, HALF_TOK)], core)]
    spread_all(1, 0)
    norm(3)
    spread_all(0, 2)
    norm(4)
    norm(5)
    nrm_swaps.append(send(nrm.at[:, second], nrm.at[:, pl.ds(TOK + HALF_TOK, HALF_TOK)], core))
    spread_all(1, 1)
    spread_all(0, 3)
    for copy in get_mv:
        copy.wait()
    for i in range(6):
        pick_send[i] = state[i][slot, 1 - s]
    moved = send(pick_send, pick_recv, pair)
    spread_all(1, 2)

    def forward(part, t):
        rows, cols = pl.ds(part * LATE, LATE), pl.ds(t * TOK, TOK)
        value, rate = gelu_both(dot(w1[rows, :], nrm[:, cols], 1, 0))
        act[rows, cols] = value.astype(BF16)
        gate[rows, cols] = rate

    def backward(part):
        @pl.loop(0, 2)
        def _(t):
            rows, cols = pl.ds(part * LATE, LATE), pl.ds(pl.multiple_of(t * TOK, 128), TOK)
            back = dot(w2[rows, :], og[:, cols], 1, 0)
            slope[rows, cols] = (back * gate[rows, cols]).astype(BF16)

    def branch(block):
        return dot(w2[...], act[:, pl.ds(block * HALF_TOK, HALF_TOK)], 0, 0)

    sums = {}
    grads = (gd, gu)
    early, late = pl.ds(0, LATE), pl.ds(LATE, LATE)

    def rows_of(j, q):
        return pl.ds(q * 256 + (240 if j < 0 else (16 - (2 << j)) * ROWS), ROWS if j < 0 else ROWS << j)

    def ship(g, q, j, value):
        rows, k = rows_of(j, q), 5 * q + j + 1
        to = xy[(q + j) % 4] if j >= 0 else zs[q - 1]
        encode(value, sum_code.at[g, rows, :], sum_scale.at[g, k])
        sums[g, q, j] = (
            send(sum_code.at[g, rows, :], sum_code_in.at[g, rows, :], to),
            send(sum_scale.at[g, k], sum_scale_in.at[g, k], to),
        )

    def arrived(g, q, j):
        for copy in sums[g, q, j]:
            copy.wait_recv()
        return decode_wide(sum_code_in.at[g, rows_of(j, q), :], sum_scale_in.at[g, 5 * q + j + 1])

    def begin(g):
        for q in range(4):
            ship(g, q, 3, grads[g][pl.ds(LATE + q * CLASS, CLASS), :])

    def advance(g, j):
        n = ROWS << j
        for q in range(4):
            rows = pl.ds(q * CLASS, n)
            value = grads[g][rows, :] + arrived(g, q, j)
            if j > 0:
                ship(g, q, j - 1, value[n // 2 :])
                grads[g][pl.ds(q * CLASS, n // 2), :] = value[: n // 2]
            elif q > 0:
                ship(g, q, -1, value)
            else:
                grads[g][rows, :] = value

    def finish(g):
        total = grads[g][pl.ds(0, ROWS), :]
        for q in (1, 2, 3):
            total = total + arrived(g, q, -1)
        return total

    forward(0, 0)
    for copy in nrm_swaps:
        copy.wait_recv()
    forward(0, 1)
    spread_all(1, 3)
    og_swap.wait_recv()
    gd[early, :] = dot(act[early, :], og[...], 1, 1)
    all_here(0, 3)
    forward(1, 0)
    forward(1, 1)
    gd[late, :] = dot(act[late, :], og[...], 1, 1)
    begin(0)
    all_here(1, 3)

    pair_swaps = {}

    def exchange(b):
        core_swaps[b].wait_recv()
        for i, cols in enumerate(tiles(HALF_TOK)):
            value = pown[b, :, cols] + precv[b, :, cols]
            encode(value, pair_code.at[b, :, cols], pair_scale.at[b, :, cols])
        pair_swaps[b] = (
            send(pair_code.at[b], pair_code_in.at[1 - b], pair),
            send(pair_scale.at[b], pair_scale_in.at[1 - b], pair),
        )

    def complete(b, where, sem):
        for copy in pair_swaps[1 - b]:
            copy.wait_recv()
        for cols in tiles(HALF_TOK):
            at = pl.ds(b * HALF_TOK + cols.start, 128)
            near = decode(pair_code.at[b, :, cols], pair_scale.at[b, :, cols], pl.ds(0, 128))
            far = decode(pair_code_in.at[b, :, cols], pair_scale_in.at[b, :, cols], pl.ds(0, 128))
            mix[b, :, cols] = (tok[:, at].astype(F32) + (near + far)).astype(BF16)
        put = pltpu.make_async_copy(mix.at[b], mixed_out.at[:, where], local_sem.at[sem])
        put.start()
        return put

    core_swaps = {}
    psend[1] = branch(3)
    core_swaps[1] = send(psend.at[1], precv.at[1], core)
    pown[1] = branch(1)
    backward(1)
    exchange(1)
    gu[late, :] = dot(slope[late, :], nrm[...], 1, 1)
    begin(1)
    psend[0] = branch(2)
    core_swaps[0] = send(psend.at[0], precv.at[0], core)
    advance(0, 3)
    pown[0] = branch(0)
    exchange(0)
    backward(0)
    advance(0, 2)
    gu[early, :] = dot(slope[early, :], nrm[...], 1, 1)
    advance(0, 1)
    advance(1, 3)
    advance(0, 0)
    advance(1, 2)
    moved.wait_recv()
    for i in range(6):
        picked[i] = jnp.where(owner == s, state[i][slot, s], pick_recv[i])
    advance(1, 1)
    puts = [complete(0, mine, 11)]
    advance(1, 0)
    fresh[3], fresh[4], fresh[5] = adam_update(picked[1], picked[3], picked[5], finish(0))
    fresh[0], fresh[1], fresh[2] = adam_update(picked[0], picked[2], picked[4], finish(1))
    puts.append(pltpu.make_async_copy(fresh, state_out, local_sem.at[12]))
    puts[1].start()
    puts.append(complete(1, other, 10))
    for copy in puts:
        copy.wait()
    for copy in started:
        copy.wait_send()


COPIES = 2 + 6 + 1 + 2 + 1 + 80 + 2 + 4 + 2 * 38


def hand_out(mixed_in, state_in, mixed_out, *rest):
    outs, (mixed, state, sem) = rest[:6], rest[6:]
    bands = [pl.ds(i * D // 4, D // 4) for i in range(4)]
    gets = [pltpu.make_async_copy(mixed_in.at[band, :], mixed.at[band, :], sem.at[i]) for i, band in enumerate(bands)]
    gets.append(pltpu.make_async_copy(state_in, state, sem.at[4]))
    puts = [[pltpu.make_async_copy(mixed.at[band, :], mixed_out.at[band, :], sem.at[5 + i])] for i, band in enumerate(bands)]
    puts.append([pltpu.make_async_copy(state.at[i], outs[i], sem.at[9 + i]) for i in range(6)])
    for get in gets:
        get.start()
    for get, put in zip(gets, puts):
        get.wait()
        for copy in put:
            copy.start()
    for put in puts:
        for copy in put:
            copy.wait()


def local(tokens, out_grad, boundary, up_old, down_old, up_mom, up_var, down_mom, down_var):
    layers = up_old.shape[0]
    hbm = pl.BlockSpec(memory_space=pl.ANY)
    swap = lambda a: jnp.swapaxes(a, -1, -2)
    V = pltpu.VMEM
    mixed_type = jax.ShapeDtypeStruct((D, TOK), BF16)
    results = pl.pallas_call(
        kernel,
        out_shape=[mixed_type, jax.ShapeDtypeStruct((6, ROWS, D), F32)],
        in_specs=[pl.BlockSpec(memory_space=pltpu.SMEM)] + [hbm] * 8,
        out_specs=[hbm] * 2,
        scratch_shapes=[
            *[V((layers, 2, ROWS, D), F32)] * 6,
            V((2, 2, ROWS, D), BF16),
            V((2, ROWS, D), BF16),
            V((6, ROWS, D), F32),
            V((6, ROWS, D), F32),
            V((6, ROWS, D), F32),
            V((6, ROWS, D), F32),
            V((D, TOK), BF16),
            V((D, 2 * TOK), BF16),
            V((D, 2 * TOK), BF16),
            V((UNITS, D), BF16),
            V((UNITS, D), BF16),
            V((UNITS, 2 * TOK), BF16),
            V((UNITS, 2 * TOK), F32),
            V((UNITS, 2 * TOK), BF16),
            V((2, D, HALF_TOK), F32),
            V((2, D, HALF_TOK), F32),
            V((2, D, HALF_TOK), F32),
            *[V((2, D, HALF_TOK), jnp.int16), V((2, 8, HALF_TOK), F32)] * 2,
            V((2, D, HALF_TOK), BF16),
            V((UNITS, D), F32),
            V((UNITS, D), F32),
            *[V((2, 4 * 256, D), jnp.int16), V((2, 20, 8, 128), F32)] * 2,
            pltpu.SemaphoreType.DMA((13,)),
            pltpu.SemaphoreType.DMA((COPIES,)),
            pltpu.SemaphoreType.DMA((COPIES,)),
        ],
        compiler_params=pltpu.CompilerParams(
            collective_id=0, has_side_effects=True, vmem_limit_bytes=60 * 2**20
        ),
        name="block_step",
    )(
        boundary,
        swap(tokens),
        swap(out_grad),
        swap(up_old),
        down_old,
        swap(up_mom),
        swap(up_var),
        down_mom,
        down_var,
    )
    mixed, up_w, up_m, up_v, down_w, down_m, down_v = pl.pallas_call(
        hand_out,
        out_shape=[mixed_type] + [jax.ShapeDtypeStruct((ROWS, D), F32)] * 6,
        in_specs=[hbm] * 2,
        out_specs=[hbm] * 7,
        scratch_shapes=[V((D, TOK), BF16), V((6, ROWS, D), F32), pltpu.SemaphoreType.DMA((15,))],
        compiler_params=pltpu.CompilerParams(vmem_limit_bytes=60 * 2**20),
        name="hand_out",
    )(*results)
    return (
        swap(mixed),
        swap(up_w)[None],
        swap(up_m)[None],
        swap(up_v)[None],
        down_w[None],
        down_m[None],
        down_v[None],
    )


def solution(mesh):
    in_specs = (
        P("dp", None),
        P("dp", None),
        P(),
        P("section", None, None, "dp"),
        P("section", None, "dp", None),
        P("section", None, None, "dp"),
        P("section", None, None, "dp"),
        P("section", None, "dp", None),
        P("section", None, "dp", None),
    )
    out_specs = (
        P("dp", None),
        P("section", None, "dp"),
        P("section", None, "dp"),
        P("section", None, "dp"),
        P("section", "dp", None),
        P("section", "dp", None),
        P("section", "dp", None),
    )
    return jax.shard_map(local, mesh=mesh, in_specs=in_specs, out_specs=out_specs, check_vma=False)
```

```python
import functools
import math

import jax
import jax.numpy as jnp
from jax import lax
from jax.experimental import pallas as pl
from jax.experimental.pallas import tpu as pltpu
from jax.sharding import PartitionSpec as P

root_half = 1.0 / math.sqrt(2.0)
root_circle = 1.0 / math.sqrt(2.0 * math.pi)
first_fix = 1.0 - 0.9**10
second_fix = 1.0 - 0.999**10

D = 832
ROWS = 16
TOK = 768
HALF_TOK = TOK // 2
UNITS = 64 * ROWS
CLASS = 8 * ROWS
LATE = UNITS // 2
F32 = jnp.float32
BF16 = jnp.bfloat16


def dot(a, b, ca, cb):
    return lax.dot_general(a, b, (((ca,), (cb,)), ((), ())), preferred_element_type=F32)


def gelu_both(value):
    both = 1.0 + lax.erf(value * root_half)
    return 0.5 * value * both, 0.5 * both + value * jnp.exp(-0.5 * value * value) * root_circle


def layer_norm(tokens):
    wide = tokens.astype(F32)
    center = wide - jnp.mean(wide, axis=0, keepdims=True)
    spread = jnp.mean(center * center, axis=0, keepdims=True)
    return (center * lax.rsqrt(spread + 1e-06)).astype(BF16)


def adam_update(weight, moment, second, grad):
    moment_new = 0.9 * moment + 0.1 * grad
    second_new = 0.999 * second + 0.001 * grad * grad
    stride = moment_new / first_fix / (jnp.sqrt(second_new / second_fix) + 1e-08)
    return (weight - 0.001 * stride, moment_new, second_new)


def tiles(width):
    return [pl.ds(at, min(128, width - at)) for at in range(0, width, 128)]


def encode(x, code, scale):
    n, w = x.shape
    top = jnp.max(jnp.abs(x).reshape(n // 8, 8, w), axis=0)
    best = top[:, :128]
    for at in range(128, w - 127, 128):
        best = jnp.maximum(best, top[:, at : at + 128])
    rest = w % 128
    if rest:
        best = jnp.concatenate([jnp.maximum(best[:, :rest], top[:, w - rest :]), best[:, rest:]], axis=1)
    unit = jnp.maximum(best, 1e-30) * (1.0 / 32760.0)
    scale[...] = unit
    per = 1.0 / unit
    for cols in tiles(w):
        part = x[:, cols.start : cols.start + cols.size].reshape(n // 8, 8, cols.size)
        part = jnp.round(part * per[None, :, : cols.size])
        code[:, cols] = part.astype(jnp.int32).astype(jnp.int16).reshape(n, cols.size)


def decode(code, scale, cols):
    part = code[:, cols].astype(jnp.int32).astype(F32)
    n, w = part.shape
    return (part.reshape(n // 8, 8, w) * scale[:, pl.ds(0, w)][None]).reshape(n, w)


def decode_wide(code, scale):
    return jnp.concatenate([decode(code, scale, cols) for cols in tiles(code.shape[1])], axis=1)


def flip1(v):
    return v + 1 - 2 * lax.rem(v, 2)


def flip2(v):
    return lax.rem(v + 2, 4)


def flip3(v):
    return 3 - v


def kernel(
    boundary,
    tok_in,
    og_in,
    up_w_in,
    down_w_in,
    up_m_in,
    up_v_in,
    down_m_in,
    down_v_in,
    mixed_out,
    state_out,
    up_w,
    down_w,
    up_m,
    down_m,
    up_v,
    down_v,
    bpiece,
    brecv,
    pick_send,
    pick_recv,
    picked,
    fresh,
    tok,
    nrm,
    og,
    w1,
    w2,
    act,
    gate,
    slope,
    psend,
    pown,
    precv,
    pair_code,
    pair_scale,
    pair_code_in,
    pair_scale_in,
    mix,
    gd,
    gu,
    sum_code,
    sum_scale,
    sum_code_in,
    sum_scale_in,
    local_sem,
    send_sem,
    recv_sem,
):
    s = lax.axis_index("section")
    d = lax.axis_index("dp")
    x, y, z, c = lax.div(d, 32), lax.rem(lax.div(d, 8), 4), lax.rem(lax.div(d, 2), 4), lax.rem(d, 2)
    core = {"dp": d + 1 - 2 * c}
    pair = {"section": 1 - s}
    xy = (
        {"dp": d + (flip1(x) - x) * 32},
        {"dp": d + (flip3(x) - x) * 32},
        {"dp": d + (flip1(y) - y) * 8},
        {"dp": d + (flip3(y) - y) * 8},
    )
    zs = (
        {"dp": d + (flip1(z) - z) * 2},
        {"dp": d + (flip3(z) - z) * 2},
        {"dp": d + (flip2(z) - z) * 2},
    )
    state = (up_w, down_w, up_m, down_m, up_v, down_v)
    active = boundary[0]
    slot = lax.rem(active, 6)
    owner = lax.div(active, 6)

    count = [0]
    started = []

    def send(src, dst, dev):
        i = count[0]
        count[0] += 1
        copy = pltpu.make_async_remote_copy(
            src_ref=src,
            dst_ref=dst,
            send_sem=send_sem.at[i],
            recv_sem=recv_sem.at[i],
            device_id=dev,
            device_id_type=pl.DeviceIdType.MESH,
        )
        copy.start()
        started.append(copy)
        return copy

    mine = pl.ds(pl.multiple_of(s * HALF_TOK, 128), HALF_TOK)
    other = pl.ds(pl.multiple_of((1 - s) * HALF_TOK, 128), HALF_TOK)
    first, second = pl.ds(0, HALF_TOK), pl.ds(HALF_TOK, HALF_TOK)

    def fetch(i, src, dst):
        copy = pltpu.make_async_copy(src, dst, local_sem.at[i])
        copy.start()
        return copy

    get_w = [fetch(0, up_w_in, up_w), fetch(1, down_w_in, down_w)]
    barrier = pltpu.get_barrier_semaphore()
    peers = (core, pair) + xy + zs
    for peer in peers:
        pl.semaphore_signal(barrier, inc=1, device_id=peer, device_id_type=pl.DeviceIdType.MESH)
    get_tok = [
        fetch(2, tok_in.at[:, mine], tok.at[:, first]),
        fetch(3, tok_in.at[:, other], tok.at[:, second]),
    ]
    get_og = [
        fetch(4, og_in.at[:, mine], og.at[:, first]),
        fetch(5, og_in.at[:, other], og.at[:, second]),
    ]
    get_mv = [
        fetch(6, up_m_in, up_m),
        fetch(7, down_m_in, down_m),
        fetch(8, up_v_in, up_v),
        fetch(9, down_v_in, down_v),
    ]

    def norm(i):
        at = pl.ds(i * 128, 128)
        nrm[:, at] = layer_norm(tok[:, at])

    for copy in get_w:
        copy.wait()
    for m in (0, 1):
        bpiece[0, m] = state[m][slot, s].astype(BF16)
        bpiece[1, m] = state[m][slot, 1 - s].astype(BF16)
    pl.semaphore_wait(barrier, len(peers))
    offers = [send(bpiece.at[1, m], brecv.at[m], pair) for m in (0, 1)]
    for copy in get_tok:
        copy.wait()
    weights = (w1, w2)
    gathered = {}
    arrivals = {}

    def row_of(q, slot_):
        return q * CLASS + (slot_ * ROWS if slot_ < 8 else LATE + (slot_ - 8) * ROWS)

    def spread(m, q, j):
        if j == 0:
            if q > 0:
                gathered[m, q, -1].wait_recv()
            low, size = 0, 1
        else:
            low = size = 1 << (j - 1)
            for copy in arrivals[m, q, j - 1]:
                copy.wait_recv()
        for k in range(j, 4):
            copy = send(
                weights[m].at[pl.ds(row_of(q, low), size * ROWS), :],
                weights[m].at[pl.ds(row_of(q, (1 << k) + low), size * ROWS), :],
                xy[(q + k) % 4],
            )
            arrivals.setdefault((m, q, k), []).append(copy)

    def spread_all(m, j):
        for q in range(4):
            spread(m, q, j)

    def all_here(m, j):
        for q in range(4):
            for copy in arrivals[m, q, j]:
                copy.wait_recv()

    for m in (0, 1):
        offers[m].wait_recv()
        weights[m][pl.ds(0, ROWS), :] = jnp.where(owner == s, bpiece[0, m], brecv[m])
        for q in (1, 2, 3):
            gathered[m, q, -1] = send(
                weights[m].at[pl.ds(0, ROWS), :], weights[m].at[pl.ds(q * CLASS, ROWS), :], zs[q - 1]
            )
    for copy in get_og:
        copy.wait()
    og_swap = send(og.at[:, pl.ds(0, TOK)], og.at[:, pl.ds(TOK, TOK)], core)
    spread_all(0, 0)
    norm(0)
    spread_all(1, 0)
    norm(1)
    spread_all(0, 1)
    norm(2)
    nrm_swaps = [send(nrm.at[:, first], nrm.at[:, pl.ds(TOK, HALF_TOK)], core)]
    spread_all(1, 1)
    norm(3)
    spread_all(0, 2)
    norm(4)
    norm(5)
    nrm_swaps.append(send(nrm.at[:, second], nrm.at[:, pl.ds(TOK + HALF_TOK, HALF_TOK)], core))
    spread_all(1, 2)
    for copy in get_mv:
        copy.wait()
    for i in range(6):
        pick_send[i] = state[i][slot, 1 - s]
    moved = send(pick_send, pick_recv, pair)
    spread_all(0, 3)

    def forward(part, t):
        rows, cols = pl.ds(part * LATE, LATE), pl.ds(t * TOK, TOK)
        value, rate = gelu_both(dot(w1[rows, :], nrm[:, cols], 1, 0))
        act[rows, cols] = value.astype(BF16)
        gate[rows, cols] = rate

    def backward(part):
        @pl.loop(0, 2)
        def _(t):
            rows, cols = pl.ds(part * LATE, LATE), pl.ds(pl.multiple_of(t * TOK, 128), TOK)
            back = dot(w2[rows, :], og[:, cols], 1, 0)
            slope[rows, cols] = (back * gate[rows, cols]).astype(BF16)

    def branch(block, rows=pl.ds(0, UNITS)):
        return dot(w2[rows, :], act[rows, pl.ds(block * HALF_TOK, HALF_TOK)], 0, 0)

    sums = {}
    grads = (gd, gu)
    early, late = pl.ds(0, LATE), pl.ds(LATE, LATE)

    def rows_of(j, q):
        return pl.ds(q * 256 + (240 if j < 0 else (16 - (2 << j)) * ROWS), ROWS if j < 0 else ROWS << j)

    def ship(g, q, j, value):
        rows, k = rows_of(j, q), 5 * q + j + 1
        to = xy[(q + j) % 4] if j >= 0 else zs[q - 1]
        encode(value, sum_code.at[g, rows, :], sum_scale.at[g, k])
        sums[g, q, j] = (
            send(sum_code.at[g, rows, :], sum_code_in.at[g, rows, :], to),
            send(sum_scale.at[g, k], sum_scale_in.at[g, k], to),
        )

    def arrived(g, q, j):
        for copy in sums[g, q, j]:
            copy.wait_recv()
        return decode_wide(sum_code_in.at[g, rows_of(j, q), :], sum_scale_in.at[g, 5 * q + j + 1])

    def begin(g):
        for q in range(4):
            ship(g, q, 3, grads[g][pl.ds(LATE + q * CLASS, CLASS), :])

    def advance(g, j):
        n = ROWS << j
        for q in range(4):
            rows = pl.ds(q * CLASS, n)
            value = grads[g][rows, :] + arrived(g, q, j)
            if j > 0:
                ship(g, q, j - 1, value[n // 2 :])
                grads[g][pl.ds(q * CLASS, n // 2), :] = value[: n // 2]
            elif q > 0:
                ship(g, q, -1, value)
            else:
                grads[g][rows, :] = value

    def finish(g):
        total = grads[g][pl.ds(0, ROWS), :]
        for q in (1, 2, 3):
            total = total + arrived(g, q, -1)
        return total

    forward(0, 0)
    for copy in nrm_swaps:
        copy.wait_recv()
    forward(0, 1)
    spread_all(1, 3)
    og_swap.wait_recv()
    gd[early, :] = dot(act[early, :], og[...], 1, 1)
    psend[1] = branch(3, early)
    pown[1] = branch(1, early)
    all_here(0, 3)
    forward(1, 0)
    forward(1, 1)
    gd[late, :] = dot(act[late, :], og[...], 1, 1)
    begin(0)
    all_here(1, 3)

    pair_swaps = {}

    def exchange(b):
        core_swaps[b].wait_recv()
        for i, cols in enumerate(tiles(HALF_TOK)):
            value = pown[b, :, cols] + precv[b, :, cols]
            encode(value, pair_code.at[b, :, cols], pair_scale.at[b, :, cols])
        pair_swaps[b] = (
            send(pair_code.at[b], pair_code_in.at[1 - b], pair),
            send(pair_scale.at[b], pair_scale_in.at[1 - b], pair),
        )

    def complete(b, where, sem):
        for copy in pair_swaps[1 - b]:
            copy.wait_recv()
        for cols in tiles(HALF_TOK):
            at = pl.ds(b * HALF_TOK + cols.start, 128)
            near = decode(pair_code.at[b, :, cols], pair_scale.at[b, :, cols], pl.ds(0, 128))
            far = decode(pair_code_in.at[b, :, cols], pair_scale_in.at[b, :, cols], pl.ds(0, 128))
            mix[b, :, cols] = (tok[:, at].astype(F32) + (near + far)).astype(BF16)
        put = pltpu.make_async_copy(mix.at[b], mixed_out.at[:, where], local_sem.at[sem])
        put.start()
        return put

    core_swaps = {}
    psend[1] += branch(3, late)
    core_swaps[1] = send(psend.at[1], precv.at[1], core)
    pown[1] += branch(1, late)
    exchange(1)
    backward(1)
    gu[late, :] = dot(slope[late, :], nrm[...], 1, 1)
    begin(1)
    psend[0] = branch(2)
    core_swaps[0] = send(psend.at[0], precv.at[0], core)
    advance(0, 3)
    pown[0] = branch(0)
    exchange(0)
    backward(0)
    gu[early, :] = dot(slope[early, :], nrm[...], 1, 1)
    advance(1, 3)
    advance(0, 2)
    advance(1, 2)
    advance(0, 1)
    advance(1, 1)
    advance(0, 0)
    advance(1, 0)
    moved.wait_recv()
    for i in range(6):
        picked[i] = jnp.where(owner == s, state[i][slot, s], pick_recv[i])
    puts = [complete(0, mine, 11)]
    fresh[3], fresh[4], fresh[5] = adam_update(picked[1], picked[3], picked[5], finish(0))
    fresh[0], fresh[1], fresh[2] = adam_update(picked[0], picked[2], picked[4], finish(1))
    puts.append(pltpu.make_async_copy(fresh, state_out, local_sem.at[12]))
    puts[1].start()
    puts.append(complete(1, other, 10))
    for copy in puts:
        copy.wait()
    for copy in started:
        copy.wait_send()


COPIES = 2 + 6 + 1 + 2 + 1 + 80 + 2 + 4 + 2 * 38


def hand_out(mixed_in, state_in, mixed_out, *rest):
    outs, (mixed, state, sem) = rest[:6], rest[6:]
    bands = [pl.ds(i * D // 4, D // 4) for i in range(4)]
    gets = [pltpu.make_async_copy(mixed_in.at[band, :], mixed.at[band, :], sem.at[i]) for i, band in enumerate(bands)]
    gets.append(pltpu.make_async_copy(state_in, state, sem.at[4]))
    puts = [[pltpu.make_async_copy(mixed.at[band, :], mixed_out.at[band, :], sem.at[5 + i])] for i, band in enumerate(bands)]
    puts.append([pltpu.make_async_copy(state.at[i], outs[i], sem.at[9 + i]) for i in range(6)])
    for get in gets:
        get.start()
    for get, put in zip(gets, puts):
        get.wait()
        for copy in put:
            copy.start()
    for put in puts:
        for copy in put:
            copy.wait()


def local(tokens, out_grad, boundary, up_old, down_old, up_mom, up_var, down_mom, down_var):
    layers = up_old.shape[0]
    hbm = pl.BlockSpec(memory_space=pl.ANY)
    swap = lambda a: jnp.swapaxes(a, -1, -2)
    V = pltpu.VMEM
    mixed_type = jax.ShapeDtypeStruct((D, TOK), BF16)
    results = pl.pallas_call(
        kernel,
        out_shape=[mixed_type, jax.ShapeDtypeStruct((6, ROWS, D), F32)],
        in_specs=[pl.BlockSpec(memory_space=pltpu.SMEM)] + [hbm] * 8,
        out_specs=[hbm] * 2,
        scratch_shapes=[
            *[V((layers, 2, ROWS, D), F32)] * 6,
            V((2, 2, ROWS, D), BF16),
            V((2, ROWS, D), BF16),
            V((6, ROWS, D), F32),
            V((6, ROWS, D), F32),
            V((6, ROWS, D), F32),
            V((6, ROWS, D), F32),
            V((D, TOK), BF16),
            V((D, 2 * TOK), BF16),
            V((D, 2 * TOK), BF16),
            V((UNITS, D), BF16),
            V((UNITS, D), BF16),
            V((UNITS, 2 * TOK), BF16),
            V((UNITS, 2 * TOK), F32),
            V((UNITS, 2 * TOK), BF16),
            V((2, D, HALF_TOK), F32),
            V((2, D, HALF_TOK), F32),
            V((2, D, HALF_TOK), F32),
            *[V((2, D, HALF_TOK), jnp.int16), V((2, 8, HALF_TOK), F32)] * 2,
            V((2, D, HALF_TOK), BF16),
            V((UNITS, D), F32),
            V((UNITS, D), F32),
            *[V((2, 4 * 256, D), jnp.int16), V((2, 20, 8, 128), F32)] * 2,
            pltpu.SemaphoreType.DMA((13,)),
            pltpu.SemaphoreType.DMA((COPIES,)),
            pltpu.SemaphoreType.DMA((COPIES,)),
        ],
        compiler_params=pltpu.CompilerParams(
            collective_id=0, has_side_effects=True, vmem_limit_bytes=60 * 2**20
        ),
        name="block_step",
    )(
        boundary,
        swap(tokens),
        swap(out_grad),
        swap(up_old),
        down_old,
        swap(up_mom),
        swap(up_var),
        down_mom,
        down_var,
    )
    mixed, up_w, up_m, up_v, down_w, down_m, down_v = pl.pallas_call(
        hand_out,
        out_shape=[mixed_type] + [jax.ShapeDtypeStruct((ROWS, D), F32)] * 6,
        in_specs=[hbm] * 2,
        out_specs=[hbm] * 7,
        scratch_shapes=[V((D, TOK), BF16), V((6, ROWS, D), F32), pltpu.SemaphoreType.DMA((15,))],
        compiler_params=pltpu.CompilerParams(vmem_limit_bytes=60 * 2**20),
        name="hand_out",
    )(*results)
    return (
        swap(mixed),
        swap(up_w)[None],
        swap(up_m)[None],
        swap(up_v)[None],
        down_w[None],
        down_m[None],
        down_v[None],
    )


def solution(mesh):
    in_specs = (
        P("dp", None),
        P("dp", None),
        P(),
        P("section", None, None, "dp"),
        P("section", None, "dp", None),
        P("section", None, None, "dp"),
        P("section", None, None, "dp"),
        P("section", None, "dp", None),
        P("section", None, "dp", None),
    )
    out_specs = (
        P("dp", None),
        P("section", None, "dp"),
        P("section", None, "dp"),
        P("section", None, "dp"),
        P("section", "dp", None),
        P("section", "dp", None),
        P("section", "dp", None),
    )
    return jax.shard_map(local, mesh=mesh, in_specs=in_specs, out_specs=out_specs, check_vma=False)
```

```python
import functools
import math

import jax
import jax.numpy as jnp
from jax import lax
from jax.experimental import pallas as pl
from jax.experimental.pallas import tpu as pltpu
from jax.sharding import PartitionSpec as P

root_half = 1.0 / math.sqrt(2.0)
root_circle = 1.0 / math.sqrt(2.0 * math.pi)
first_fix = 1.0 - 0.9**10
second_fix = 1.0 - 0.999**10

D = 832
ROWS = 16
TOK = 768
HALF_TOK = TOK // 2
UNITS = 64 * ROWS
CLASS = 8 * ROWS
LATE = UNITS // 2
F32 = jnp.float32
BF16 = jnp.bfloat16


def dot(a, b, ca, cb):
    return lax.dot_general(a, b, (((ca,), (cb,)), ((), ())), preferred_element_type=F32)


def gelu_both(value):
    both = 1.0 + lax.erf(value * root_half)
    return 0.5 * value * both, 0.5 * both + value * jnp.exp(-0.5 * value * value) * root_circle


def layer_norm(tokens):
    wide = tokens.astype(F32)
    center = wide - jnp.mean(wide, axis=0, keepdims=True)
    spread = jnp.mean(center * center, axis=0, keepdims=True)
    return (center * lax.rsqrt(spread + 1e-06)).astype(BF16)


def adam_update(weight, moment, second, grad):
    moment_new = 0.9 * moment + 0.1 * grad
    second_new = 0.999 * second + 0.001 * grad * grad
    stride = moment_new / first_fix / (jnp.sqrt(second_new / second_fix) + 1e-08)
    return (weight - 0.001 * stride, moment_new, second_new)


def tiles(width):
    return [pl.ds(at, min(128, width - at)) for at in range(0, width, 128)]


def encode(x, code, scale):
    n, w = x.shape
    top = jnp.max(jnp.abs(x).reshape(n // 8, 8, w), axis=0)
    best = top[:, :128]
    for at in range(128, w - 127, 128):
        best = jnp.maximum(best, top[:, at : at + 128])
    rest = w % 128
    if rest:
        best = jnp.concatenate([jnp.maximum(best[:, :rest], top[:, w - rest :]), best[:, rest:]], axis=1)
    unit = jnp.maximum(best, 1e-30) * (1.0 / 32760.0)
    scale[...] = unit
    per = 1.0 / unit
    for cols in tiles(w):
        part = x[:, cols.start : cols.start + cols.size].reshape(n // 8, 8, cols.size)
        part = jnp.round(part * per[None, :, : cols.size])
        code[:, cols] = part.astype(jnp.int32).astype(jnp.int16).reshape(n, cols.size)


def decode(code, scale, cols):
    part = code[:, cols].astype(jnp.int32).astype(F32)
    n, w = part.shape
    return (part.reshape(n // 8, 8, w) * scale[:, pl.ds(0, w)][None]).reshape(n, w)


def decode_wide(code, scale):
    return jnp.concatenate([decode(code, scale, cols) for cols in tiles(code.shape[1])], axis=1)


def flip1(v):
    return v + 1 - 2 * lax.rem(v, 2)


def flip2(v):
    return lax.rem(v + 2, 4)


def flip3(v):
    return 3 - v


def kernel(
    boundary,
    tok_in,
    og_in,
    up_w_in,
    down_w_in,
    up_m_in,
    up_v_in,
    down_m_in,
    down_v_in,
    mixed_out,
    state_out,
    up_w,
    down_w,
    up_m,
    down_m,
    up_v,
    down_v,
    bpiece,
    brecv,
    pick_send,
    pick_recv,
    picked,
    fresh,
    tok,
    nrm,
    og,
    w1,
    w2,
    act,
    gate,
    slope,
    psend,
    pown,
    precv,
    pair_code,
    pair_scale,
    pair_code_in,
    pair_scale_in,
    mix,
    gd,
    gu,
    sum_code,
    sum_scale,
    sum_code_in,
    sum_scale_in,
    local_sem,
    send_sem,
    recv_sem,
):
    s = lax.axis_index("section")
    d = lax.axis_index("dp")
    x, y, z, c = lax.div(d, 32), lax.rem(lax.div(d, 8), 4), lax.rem(lax.div(d, 2), 4), lax.rem(d, 2)
    core = {"dp": d + 1 - 2 * c}
    pair = {"section": 1 - s}
    xy = (
        {"dp": d + (flip1(x) - x) * 32},
        {"dp": d + (flip3(x) - x) * 32},
        {"dp": d + (flip1(y) - y) * 8},
        {"dp": d + (flip3(y) - y) * 8},
    )
    zs = (
        {"dp": d + (flip1(z) - z) * 2},
        {"dp": d + (flip3(z) - z) * 2},
        {"dp": d + (flip2(z) - z) * 2},
    )
    state = (up_w, down_w, up_m, down_m, up_v, down_v)
    active = boundary[0]
    slot = lax.rem(active, 6)
    owner = lax.div(active, 6)

    count = [0]
    started = []

    def send(src, dst, dev):
        i = count[0]
        count[0] += 1
        copy = pltpu.make_async_remote_copy(
            src_ref=src,
            dst_ref=dst,
            send_sem=send_sem.at[i],
            recv_sem=recv_sem.at[i],
            device_id=dev,
            device_id_type=pl.DeviceIdType.MESH,
        )
        copy.start()
        started.append(copy)
        return copy

    mine = pl.ds(pl.multiple_of(s * HALF_TOK, 128), HALF_TOK)
    other = pl.ds(pl.multiple_of((1 - s) * HALF_TOK, 128), HALF_TOK)
    first, second = pl.ds(0, HALF_TOK), pl.ds(HALF_TOK, HALF_TOK)

    def fetch(i, src, dst):
        copy = pltpu.make_async_copy(src, dst, local_sem.at[i])
        copy.start()
        return copy

    get_w = [fetch(0, up_w_in, up_w), fetch(1, down_w_in, down_w)]
    barrier = pltpu.get_barrier_semaphore()
    peers = (core, pair) + xy + zs
    for peer in peers:
        pl.semaphore_signal(barrier, inc=1, device_id=peer, device_id_type=pl.DeviceIdType.MESH)
    get_tok = [
        fetch(2, tok_in.at[:, mine], tok.at[:, first]),
        fetch(3, tok_in.at[:, other], tok.at[:, second]),
    ]
    get_og = [
        fetch(4, og_in.at[:, mine], og.at[:, first]),
        fetch(5, og_in.at[:, other], og.at[:, second]),
    ]
    get_mv = [
        fetch(6, up_m_in, up_m),
        fetch(7, down_m_in, down_m),
        fetch(8, up_v_in, up_v),
        fetch(9, down_v_in, down_v),
    ]

    def norm(i):
        at = pl.ds(i * 128, 128)
        nrm[:, at] = layer_norm(tok[:, at])

    for copy in get_w:
        copy.wait()
    for m in (0, 1):
        bpiece[0, m] = state[m][slot, s].astype(BF16)
        bpiece[1, m] = state[m][slot, 1 - s].astype(BF16)
    pl.semaphore_wait(barrier, len(peers))
    offers = [send(bpiece.at[1, m], brecv.at[m], pair) for m in (0, 1)]
    for copy in get_tok:
        copy.wait()
    weights = (w1, w2)
    gathered = {}
    arrivals = {}

    def row_of(q, slot_):
        return q * CLASS + (slot_ * ROWS if slot_ < 8 else LATE + (slot_ - 8) * ROWS)

    def spread(m, q, j):
        if j == 0:
            if q > 0:
                gathered[m, q, -1].wait_recv()
            low, size = 0, 1
        else:
            low = size = 1 << (j - 1)
            for copy in arrivals[m, q, j - 1]:
                copy.wait_recv()
        for k in range(j, 4):
            copy = send(
                weights[m].at[pl.ds(row_of(q, low), size * ROWS), :],
                weights[m].at[pl.ds(row_of(q, (1 << k) + low), size * ROWS), :],
                xy[(q + k) % 4],
            )
            arrivals.setdefault((m, q, k), []).append(copy)

    def spread_all(m, j):
        for q in range(4):
            spread(m, q, j)

    def all_here(m, j):
        for q in range(4):
            for copy in arrivals[m, q, j]:
                copy.wait_recv()

    for m in (0, 1):
        offers[m].wait_recv()
        weights[m][pl.ds(0, ROWS), :] = jnp.where(owner == s, bpiece[0, m], brecv[m])
        for q in (1, 2, 3):
            gathered[m, q, -1] = send(
                weights[m].at[pl.ds(0, ROWS), :], weights[m].at[pl.ds(q * CLASS, ROWS), :], zs[q - 1]
            )
    for copy in get_og:
        copy.wait()
    og_swap = send(og.at[:, pl.ds(0, TOK)], og.at[:, pl.ds(TOK, TOK)], core)
    spread_all(0, 0)
    norm(0)
    spread_all(1, 0)
    norm(1)
    spread_all(0, 1)
    norm(2)
    nrm_swaps = [send(nrm.at[:, first], nrm.at[:, pl.ds(TOK, HALF_TOK)], core)]
    spread_all(1, 1)
    norm(3)
    spread_all(0, 2)
    norm(4)
    norm(5)
    nrm_swaps.append(send(nrm.at[:, second], nrm.at[:, pl.ds(TOK + HALF_TOK, HALF_TOK)], core))
    spread_all(1, 2)
    for copy in get_mv:
        copy.wait()
    for i in range(6):
        pick_send[i] = state[i][slot, 1 - s]
    moved = send(pick_send, pick_recv, pair)
    spread_all(0, 3)

    def forward(part, t):
        rows, cols = pl.ds(part * LATE, LATE), pl.ds(t * TOK, TOK)
        value, rate = gelu_both(dot(w1[rows, :], nrm[:, cols], 1, 0))
        act[rows, cols] = value.astype(BF16)
        gate[rows, cols] = rate

    def backward(part):
        @pl.loop(0, 2)
        def _(t):
            rows, cols = pl.ds(part * LATE, LATE), pl.ds(pl.multiple_of(t * TOK, 128), TOK)
            back = dot(w2[rows, :], og[:, cols], 1, 0)
            slope[rows, cols] = (back * gate[rows, cols]).astype(BF16)

    def branch(block, rows=pl.ds(0, UNITS)):
        return dot(w2[rows, :], act[rows, pl.ds(block * HALF_TOK, HALF_TOK)], 0, 0)

    sums = {}
    grads = (gd, gu)
    early, late = pl.ds(0, LATE), pl.ds(LATE, LATE)

    def rows_of(j, q):
        return pl.ds(q * 256 + (240 if j < 0 else (16 - (2 << j)) * ROWS), ROWS if j < 0 else ROWS << j)

    def ship(g, q, j, value):
        rows, k = rows_of(j, q), 5 * q + j + 1
        to = xy[(q + j) % 4] if j >= 0 else zs[q - 1]
        encode(value, sum_code.at[g, rows, :], sum_scale.at[g, k])
        sums[g, q, j] = (
            send(sum_code.at[g, rows, :], sum_code_in.at[g, rows, :], to),
            send(sum_scale.at[g, k], sum_scale_in.at[g, k], to),
        )

    def arrived(g, q, j):
        for copy in sums[g, q, j]:
            copy.wait_recv()
        return decode_wide(sum_code_in.at[g, rows_of(j, q), :], sum_scale_in.at[g, 5 * q + j + 1])

    def begin(g):
        for q in range(4):
            ship(g, q, 3, grads[g][pl.ds(LATE + q * CLASS, CLASS), :])

    def advance(g, j):
        n = ROWS << j
        for q in range(4):
            rows = pl.ds(q * CLASS, n)
            value = grads[g][rows, :] + arrived(g, q, j)
            if j > 0:
                ship(g, q, j - 1, value[n // 2 :])
                grads[g][pl.ds(q * CLASS, n // 2), :] = value[: n // 2]
            elif q > 0:
                ship(g, q, -1, value)
            else:
                grads[g][rows, :] = value

    def finish(g):
        total = grads[g][pl.ds(0, ROWS), :]
        for q in (1, 2, 3):
            total = total + arrived(g, q, -1)
        return total

    forward(0, 0)
    for copy in nrm_swaps:
        copy.wait_recv()
    forward(0, 1)
    spread_all(1, 3)
    og_swap.wait_recv()
    gd[early, :] = dot(act[early, :], og[...], 1, 1)
    psend[1] = branch(3, early)
    pown[1] = branch(1, early)
    all_here(0, 3)
    forward(1, 0)
    forward(1, 1)
    all_here(1, 3)

    pair_swaps = {}

    def exchange(b):
        core_swaps[b].wait_recv()
        for i, cols in enumerate(tiles(HALF_TOK)):
            value = pown[b, :, cols] + precv[b, :, cols]
            encode(value, pair_code.at[b, :, cols], pair_scale.at[b, :, cols])
        pair_swaps[b] = [send(pair_scale.at[b], pair_scale_in.at[1 - b], pair)]

    def hand_over(b, first_, count_):
        for k in range(first_, first_ + count_):
            rows = pl.ds(k * 64, 64)
            pair_swaps[b].append(send(pair_code.at[b, rows, :], pair_code_in.at[1 - b, rows, :], pair))

    def complete(b, where, sem):
        for copy in pair_swaps[1 - b]:
            copy.wait_recv()
        for cols in tiles(HALF_TOK):
            at = pl.ds(b * HALF_TOK + cols.start, 128)
            near = decode(pair_code.at[b, :, cols], pair_scale.at[b, :, cols], pl.ds(0, 128))
            far = decode(pair_code_in.at[b, :, cols], pair_scale_in.at[b, :, cols], pl.ds(0, 128))
            mix[b, :, cols] = (tok[:, at].astype(F32) + (near + far)).astype(BF16)
        put = pltpu.make_async_copy(mix.at[b], mixed_out.at[:, where], local_sem.at[sem])
        put.start()
        return put

    core_swaps = {}
    psend[1] += branch(3, late)
    core_swaps[1] = send(psend.at[1], precv.at[1], core)
    pown[1] += branch(1, late)
    gd[late, :] = dot(act[late, :], og[...], 1, 1)
    exchange(1)
    hand_over(1, 0, 13)
    begin(0)
    backward(1)
    gu[late, :] = dot(slope[late, :], nrm[...], 1, 1)
    begin(1)
    psend[0] = branch(2)
    core_swaps[0] = send(psend.at[0], precv.at[0], core)
    advance(0, 3)
    pown[0] = branch(0)
    exchange(0)
    hand_over(0, 0, 4)
    backward(0)
    gu[early, :] = dot(slope[early, :], nrm[...], 1, 1)
    advance(1, 3)
    hand_over(0, 4, 3)
    advance(0, 2)
    advance(1, 2)
    hand_over(0, 7, 3)
    advance(0, 1)
    advance(1, 1)
    hand_over(0, 10, 1)
    advance(0, 0)
    hand_over(0, 11, 1)
    advance(1, 0)
    hand_over(0, 12, 1)
    moved.wait_recv()
    for i in range(6):
        picked[i] = jnp.where(owner == s, state[i][slot, s], pick_recv[i])
    puts = [complete(0, mine, 11)]
    fresh[3], fresh[4], fresh[5] = adam_update(picked[1], picked[3], picked[5], finish(0))
    fresh[0], fresh[1], fresh[2] = adam_update(picked[0], picked[2], picked[4], finish(1))
    puts.append(pltpu.make_async_copy(fresh, state_out, local_sem.at[12]))
    puts[1].start()
    puts.append(complete(1, other, 10))
    for copy in puts:
        copy.wait()
    for copy in started:
        copy.wait_send()


COPIES = 24 + 2 + 6 + 1 + 2 + 1 + 80 + 2 + 4 + 2 * 38


def hand_out(mixed_in, state_in, mixed_out, *rest):
    outs, (mixed, state, sem) = rest[:6], rest[6:]
    bands = [pl.ds(i * D // 4, D // 4) for i in range(4)]
    gets = [pltpu.make_async_copy(mixed_in.at[band, :], mixed.at[band, :], sem.at[i]) for i, band in enumerate(bands)]
    gets.append(pltpu.make_async_copy(state_in, state, sem.at[4]))
    puts = [[pltpu.make_async_copy(mixed.at[band, :], mixed_out.at[band, :], sem.at[5 + i])] for i, band in enumerate(bands)]
    puts.append([pltpu.make_async_copy(state.at[i], outs[i], sem.at[9 + i]) for i in range(6)])
    for get in gets:
        get.start()
    for get, put in zip(gets, puts):
        get.wait()
        for copy in put:
            copy.start()
    for put in puts:
        for copy in put:
            copy.wait()


def local(tokens, out_grad, boundary, up_old, down_old, up_mom, up_var, down_mom, down_var):
    layers = up_old.shape[0]
    hbm = pl.BlockSpec(memory_space=pl.ANY)
    swap = lambda a: jnp.swapaxes(a, -1, -2)
    V = pltpu.VMEM
    mixed_type = jax.ShapeDtypeStruct((D, TOK), BF16)
    results = pl.pallas_call(
        kernel,
        out_shape=[mixed_type, jax.ShapeDtypeStruct((6, ROWS, D), F32)],
        in_specs=[pl.BlockSpec(memory_space=pltpu.SMEM)] + [hbm] * 8,
        out_specs=[hbm] * 2,
        scratch_shapes=[
            *[V((layers, 2, ROWS, D), F32)] * 6,
            V((2, 2, ROWS, D), BF16),
            V((2, ROWS, D), BF16),
            V((6, ROWS, D), F32),
            V((6, ROWS, D), F32),
            V((6, ROWS, D), F32),
            V((6, ROWS, D), F32),
            V((D, TOK), BF16),
            V((D, 2 * TOK), BF16),
            V((D, 2 * TOK), BF16),
            V((UNITS, D), BF16),
            V((UNITS, D), BF16),
            V((UNITS, 2 * TOK), BF16),
            V((UNITS, 2 * TOK), F32),
            V((UNITS, 2 * TOK), BF16),
            V((2, D, HALF_TOK), F32),
            V((2, D, HALF_TOK), F32),
            V((2, D, HALF_TOK), F32),
            *[V((2, D, HALF_TOK), jnp.int16), V((2, 8, HALF_TOK), F32)] * 2,
            V((2, D, HALF_TOK), BF16),
            V((UNITS, D), F32),
            V((UNITS, D), F32),
            *[V((2, 4 * 256, D), jnp.int16), V((2, 20, 8, 128), F32)] * 2,
            pltpu.SemaphoreType.DMA((13,)),
            pltpu.SemaphoreType.DMA((COPIES,)),
            pltpu.SemaphoreType.DMA((COPIES,)),
        ],
        compiler_params=pltpu.CompilerParams(
            collective_id=0, has_side_effects=True, vmem_limit_bytes=60 * 2**20
        ),
        name="block_step",
    )(
        boundary,
        swap(tokens),
        swap(out_grad),
        swap(up_old),
        down_old,
        swap(up_mom),
        swap(up_var),
        down_mom,
        down_var,
    )
    mixed, up_w, up_m, up_v, down_w, down_m, down_v = pl.pallas_call(
        hand_out,
        out_shape=[mixed_type] + [jax.ShapeDtypeStruct((ROWS, D), F32)] * 6,
        in_specs=[hbm] * 2,
        out_specs=[hbm] * 7,
        scratch_shapes=[V((D, TOK), BF16), V((6, ROWS, D), F32), pltpu.SemaphoreType.DMA((15,))],
        compiler_params=pltpu.CompilerParams(vmem_limit_bytes=60 * 2**20),
        name="hand_out",
    )(*results)
    return (
        swap(mixed),
        swap(up_w)[None],
        swap(up_m)[None],
        swap(up_v)[None],
        down_w[None],
        down_m[None],
        down_v[None],
    )


def solution(mesh):
    in_specs = (
        P("dp", None),
        P("dp", None),
        P(),
        P("section", None, None, "dp"),
        P("section", None, "dp", None),
        P("section", None, None, "dp"),
        P("section", None, None, "dp"),
        P("section", None, "dp", None),
        P("section", None, "dp", None),
    )
    out_specs = (
        P("dp", None),
        P("section", None, "dp"),
        P("section", None, "dp"),
        P("section", None, "dp"),
        P("section", "dp", None),
        P("section", "dp", None),
        P("section", "dp", None),
    )
    return jax.shard_map(local, mesh=mesh, in_specs=in_specs, out_specs=out_specs, check_vma=False)
```
